32 devices in a mesh: expert: 8 (over z, core), dp: 4 (over y, x).
Axes of the slice: x: 2, y: 2, z: 4, core: 2. Of those that a mesh axis runs over, the one named last changes fastest.
Arguments:
- hidden_rows: bfloat16 [4, 4096, 768], P('dp', 'expert'), may hold values from -5 to 5
- grad_send: bfloat16 [4, 4096, 2048], P('dp', 'expert'), may hold values from -5 to 5
- row_index: int32 [8, 512], P('expert'), may hold values from 0 to 511, each once within a row
- block_expert: int32 [8, 4], P('expert'), may hold values from 0 to 1
- block_count: int32 [8, 4], P('expert'), may hold values from 1 to 128
- down_weight: bfloat16 [16, 768, 2048], P('expert', None, 'dp'), may hold values from -0.21875 to 0.21875
Outputs:
- grad_hidden: bfloat16 [4, 4096, 768], P('dp', 'expert')
- new_weight: bfloat16 [16, 768, 2048], P('expert', None, 'dp')
The draws below stay inside these ranges and needn't reach their ends.
Inputs may be any that keep to these rules, and one draw needn't show every extreme that they name: Each row of row_index is a permutation of 0 to 511.
All inputs are finite; a program needn't handle non-finite values.
Results may differ from the reference program's by a relative error of at most 0.0085.
Values may be sent and summed in bfloat16 or wider, within the bound.
A program may use at most 128 MiB of HBM per device.

```python
import jax
import jax.numpy as jnp
import numpy as np
from jax import lax

D = 2048
FF = 768
EXP_DEV = 2
ROWS = 512
BLOCK = 128
CAP = 64
NBLK = 4
EXPERTS = 16
N_EXPERT = 8
N_DP = 4


def draw_hidden_rows(key, part):
    key = jax.random.fold_in(key, 11)
    key_common, key_own = jax.random.split(key)
    shape = (N_DP, N_EXPERT * ROWS, FF)
    common = jax.random.normal(key_common, (1, N_EXPERT * ROWS, FF), jnp.float32)
    own_part = jax.random.normal(key_own, shape, jnp.float32)
    mixed = 0.8 * common + 0.6 * own_part
    return jnp.clip(mixed, -5.0, 5.0).astype(jnp.bfloat16)


def draw_grad_send(key, part):
    key = jax.random.fold_in(key, 12)
    key_common, key_own = jax.random.split(key)
    shape = (N_DP, N_EXPERT * ROWS, D)
    column = jnp.arange(D).astype(jnp.float32) / float(D - 1)
    col_scale = 0.5 * jnp.exp(1.6094 * column)
    shared = 0.15 + 0.8 * column
    private = jnp.sqrt(1.0 - shared * shared)
    common = jax.random.normal(key_common, (1, N_EXPERT * ROWS, D), jnp.float32)
    own_part = jax.random.normal(key_own, shape, jnp.float32)
    mixed = col_scale * (shared * common + private * own_part)
    return jnp.clip(mixed, -5.0, 5.0).astype(jnp.bfloat16)


def with_ends(array, key, low, high):
    shape = array.shape
    index_at = [jax.random.randint(jax.random.fold_in(key, axis), (), 0, shape[axis]) for axis in range(len(shape))]
    array = array.at[tuple(index_at)].set(low)
    longest = shape.index(max(shape))
    index_at[longest] = (index_at[longest] + 1) % shape[longest]
    return array.at[tuple(index_at)].set(high)


def shard_levels(own_key, extent, cuts, smallest, top_value):
    loudness = 1.0
    for dim, parts in cuts:
        steps = jax.random.uniform(jax.random.fold_in(jax.random.fold_in(own_key, 6), dim), (parts,), jnp.float32, smallest / len(cuts), top_value / len(cuts))
        loudness = loudness * jnp.repeat(jnp.exp(steps), extent[dim] // parts).reshape((-1,) + (1,) * (len(extent) - 1 - dim))
    return loudness


def normal_values(stream_key, extent, scale, most, shards=(), kind=jnp.bfloat16):
    values = scale * jax.random.normal(stream_key, extent, jnp.float32)
    if shards:
        values = values * shard_levels(stream_key, extent, shards, -0.22, 0.18)
    return jnp.clip(values, -most, most).astype(kind)


def setup_inputs(seed: int = 0) -> dict:
    key_list = jax.random.split(jax.random.key(seed), 7)
    hidden_rows = draw_hidden_rows(jax.random.fold_in(key_list[6], 71), 0)
    grad_send = draw_grad_send(jax.random.fold_in(key_list[6], 71), 0)
    row_index = jax.vmap(lambda own: jax.random.permutation(own, ROWS))(jax.random.split(key_list[2], N_EXPERT)).reshape((N_EXPERT, ROWS)).astype(jnp.int32)
    block_expert = with_ends(jax.random.randint(key_list[3], (N_EXPERT, NBLK), 0, EXP_DEV), jax.random.fold_in(key_list[3], 1), 0, EXP_DEV - 1).astype(jnp.int32)
    block_count = with_ends(jax.random.randint(key_list[4], (N_EXPERT, NBLK), 1, BLOCK + 1), jax.random.fold_in(key_list[4], 1), 1, BLOCK).astype(jnp.int32)
    down_weight = normal_values(key_list[5], (EXPERTS, FF, D), FF ** -0.5, 0.21875, ((0, 8), (2, 4)))
    return dict(hidden_rows=hidden_rows, grad_send=grad_send, row_index=row_index, block_expert=block_expert, block_count=block_count, down_weight=down_weight)


learn_rate = 0.01
epsilon = 1e-6


def one_device(operands):
    arrived, hidden, indices, block_map, block_fill, weights = operands
    gathered = jnp.take(arrived, indices, axis=1)
    position = jnp.arange(ROWS)
    block_of = position // BLOCK
    live_rows = (position % BLOCK) < jnp.take(block_fill, block_of)
    slot_expert = jnp.take(block_map, block_of)
    masked = jnp.where(live_rows[None, :, None], gathered, jnp.zeros_like(gathered))
    chosen = jnp.take(weights, block_map, axis=0).astype(jnp.float32)
    grad_blocks = masked.reshape(N_DP, NBLK, BLOCK, D).astype(jnp.float32)
    grad_hidden = jnp.einsum("inbd,nfd->inbf", grad_blocks, chosen).reshape(N_DP, ROWS, FF).astype(jnp.bfloat16)
    pieces = []
    for expert in range(EXP_DEV):
        selected = jnp.where((slot_expert == expert)[None, :, None], hidden, jnp.zeros_like(hidden))
        pieces.append(jnp.einsum("irf,ird->ifd", selected.astype(jnp.float32), masked.astype(jnp.float32)))
    vector = jnp.stack(pieces, axis=1).astype(jnp.bfloat16)
    levels = N_DP.bit_length() - 1
    for halving in range(levels):
        bit_no = levels - 1 - halving
        partner = jnp.asarray(np.arange(N_DP) ^ (1 << bit_no), jnp.int32)
        own_part = vector.astype(jnp.float32)
        other_part = jnp.take(own_part, partner, axis=0)
        inner = jnp.sum(own_part * other_part, axis=(2, 3))
        norm_own = jnp.sum(own_part * own_part, axis=(2, 3))
        norm_other = jnp.take(norm_own, partner, axis=0)
        coef_own = 1.0 - inner / (2.0 * (norm_own + epsilon))
        coef_other = 1.0 - inner / (2.0 * (norm_other + epsilon))
        vector = (coef_own[:, :, None, None] * own_part + coef_other[:, :, None, None] * other_part).astype(jnp.bfloat16)
    updated = (weights.astype(jnp.float32) - learn_rate * vector[0].astype(jnp.float32)).astype(jnp.bfloat16)
    return grad_hidden, updated


def reference(hidden_rows, grad_send, row_index, block_expert, block_count, down_weight):
    arrived = grad_send.reshape(N_DP, N_EXPERT, N_EXPERT, CAP, D).transpose(2, 0, 1, 3, 4).reshape(N_EXPERT, N_DP, ROWS, D)
    hidden = hidden_rows.reshape(N_DP, N_EXPERT, ROWS, FF).transpose(1, 0, 2, 3)
    weights = down_weight.reshape(N_EXPERT, EXP_DEV, FF, D)
    grad_hidden, updated = lax.map(one_device, (arrived, hidden, row_index, block_expert, block_count, weights))
    grad_hidden = grad_hidden.transpose(1, 0, 2, 3).reshape(N_DP, N_EXPERT * ROWS, FF)
    return grad_hidden, updated.reshape(EXPERTS, FF, D)
```

```python
import functools

import jax
import jax.numpy as jnp
from jax import lax
from jax.experimental import pallas as pl
from jax.experimental.pallas import tpu as pltpu
from jax.sharding import PartitionSpec as P

learn_rate = 0.01
epsilon = 1e-06
MESH = pl.DeviceIdType.MESH
bf16 = jnp.bfloat16
f32 = jnp.float32


def kernel(
    n_e,
    n,
    grad_ref,
    hidden_ref,
    index_ref,
    expert_ref,
    count_ref,
    w_ref,
    gh_ref,
    nw_ref,
    arrived,
    part,
    pick,
    hall,
    outp,
    inp,
    v,
    stat,
    stat_in,
    z_send,
    z_recv,
    m_send,
    m_recv,
    h_send,
    h_recv,
    p_send,
    p_recv,
    s_send,
    s_recv,
    own_sem,
):
    rows, ff = hidden_ref.shape
    cap = arrived.shape[1]
    local, _, cols = w_ref.shape
    blocks = expert_ref.shape[0]
    block = rows // blocks
    me_e, me = lax.axis_index("expert"), lax.axis_index("dp")

    def near_e(k):
        return lax.rem(me_e + k + n_e, n_e)

    def near(k):
        return lax.rem(me + k + n, n)

    barrier = pltpu.get_barrier_semaphore()
    for k in range(1, n_e):
        pl.semaphore_signal(barrier, inc=1, device_id={"expert": near_e(k)}, device_id_type=MESH)
    for k in range(1, n):
        pl.semaphore_signal(barrier, inc=1, device_id={"dp": near(k)}, device_id_type=MESH)
    own = pltpu.make_async_copy(grad_ref.at[pl.ds(me_e * cap, cap)], arrived.at[me_e], own_sem)
    own.start()
    pl.semaphore_wait(barrier, n_e + n - 2)

    order = sorted(range(1, n_e), key=lambda k: -min(k, n_e - k))
    z_copies = {}
    for k in order:
        to = near_e(k)
        z_copies[k] = pltpu.make_async_remote_copy(
            src_ref=grad_ref.at[pl.ds(to * cap, cap)],
            dst_ref=arrived.at[me_e],
            send_sem=z_send.at[k - 1],
            recv_sem=z_recv.at[k - 1],
            device_id={"expert": to},
            device_id_type=MESH,
        )
        z_copies[k].start()
    h_copies = []
    for k in range(1, n):
        copy = pltpu.make_async_remote_copy(
            src_ref=hidden_ref,
            dst_ref=hall.at[k - 1],
            send_sem=h_send.at[k - 1],
            recv_sem=h_recv.at[k - 1],
            device_id={"dp": near(k)},
            device_id_type=MESH,
        )
        copy.start()
        h_copies.append(copy)

    for b in range(blocks):
        span = pl.ds(b * block, block)
        slot = lax.broadcasted_iota(jnp.int32, (block, rows), 0)
        row = lax.broadcasted_iota(jnp.int32, (block, rows), 1)
        hit = (index_ref[span, :] == row) & (slot < count_ref[b])
        pick[span, :] = jnp.where(hit, 1.0, 0.0).astype(bf16)

    def forward(source):
        for k in range(1, n):
            to = near(k)
            pltpu.make_async_remote_copy(
                src_ref=arrived.at[source, :, pl.ds(pl.multiple_of(to * cols, cols), cols)],
                dst_ref=part.at[k, source],
                send_sem=m_send.at[k - 1],
                recv_sem=m_recv.at[k - 1],
                device_id={"dp": to},
                device_id_type=MESH,
            ).start()

    own.wait()
    forward(me_e)
    for k in [1] + [k for k in order if k != 1]:
        z_copies[k].wait_recv()
        forward(near_e(-k))

    def slots(k):
        flat = part[k].reshape(rows, cols)
        return jnp.dot(pick[...], flat, preferred_element_type=f32).astype(bf16)

    def folded(k, b):
        return lax.dot_general(
            part_slots[k, pl.ds(b * block, block), :],
            w_ref[expert_ref[b]],
            (((1,), (1,)), ((), ())),
            preferred_element_type=f32,
        )

    part_slots = v["slots"]
    vec = v["vec"]

    p_copies = []
    for k in range(1, n):
        whole = pltpu.make_async_remote_copy(
            src_ref=part.at[k],
            dst_ref=part.at[k],
            send_sem=m_send.at[k - 1],
            recv_sem=m_recv.at[k - 1],
            device_id={"dp": near(k)},
            device_id_type=MESH,
        )
        whole.wait_recv()
        part_slots[k] = slots(k)
        for b in range(blocks):
            outp[k - 1, pl.ds(b * block, block), :] = folded(k, b).astype(bf16)
        copy = pltpu.make_async_remote_copy(
            src_ref=outp.at[k - 1],
            dst_ref=inp.at[k - 1],
            send_sem=p_send.at[k - 1],
            recv_sem=p_recv.at[k - 1],
            device_id={"dp": near(-k)},
            device_id_type=MESH,
        )
        copy.start()
        p_copies.append(copy)
    for s in range(n_e):
        part[0, s] = arrived[s, :, pl.ds(pl.multiple_of(me * cols, cols), cols)]
    part_slots[0] = slots(0)

    def gradient(k, hidden):
        for e in range(local):
            pieces = [
                jnp.where(expert_ref[b] == e, hidden[pl.ds(b * block, block), :], jnp.zeros((), bf16))
                for b in range(blocks)
            ]
            chosen = jnp.concatenate(pieces, axis=0)
            vec[near(-k), e] = lax.dot_general(
                chosen, part_slots[k], (((0,), (0,)), ((), ())), preferred_element_type=f32
            ).astype(bf16)

    gradient(0, hidden_ref)
    for k in range(1, n):
        h_copies[k - 1].wait_recv()
        gradient(k, hall.at[k - 1])

    tile = 64
    half = n // 2
    level = 0
    while half >= 1:
        count = half * local * 3
        for i in range(half):
            for e in range(local):

                def body(t, sums, i=i, e=e, half=half):
                    span = pl.ds(pl.multiple_of(t * tile, tile), tile)
                    a = vec[i, e, span, :].astype(f32)
                    b = vec[i + half, e, span, :].astype(f32)
                    return tuple(
                        total + jnp.sum(x.reshape(tile // 8, 8, cols), axis=0)
                        for total, x in zip(sums, (a * b, a * a, b * b))
                    )

                zero = jnp.zeros((8, cols), f32)
                sums = lax.fori_loop(0, ff // tile, body, (zero, zero, zero))
                for m in range(3):
                    narrow = sums[m][:, :128]
                    for c in range(1, cols // 128):
                        narrow = narrow + sums[m][:, c * 128 : (c + 1) * 128]
                    r = (i * local + e) * 3 + m
                    stat[level, pl.ds(r, 1), :] = jnp.sum(narrow, axis=0, keepdims=True)
        copies = []
        for k in range(1, n):
            copy = pltpu.make_async_remote_copy(
                src_ref=stat.at[level],
                dst_ref=stat_in.at[level, k - 1],
                send_sem=s_send.at[level, k - 1],
                recv_sem=s_recv.at[level, k - 1],
                device_id={"dp": near(k)},
                device_id_type=MESH,
            )
            copy.start()
            copies.append(copy)
        for copy in copies:
            copy.wait_recv()
        total = stat[level, :count, :]
        for k in range(1, n):
            total = total + stat_in[level, k - 1, :count, :]
        total = jnp.sum(total, axis=1, keepdims=True)
        for i in range(half):
            for e in range(local):
                r = (i * local + e) * 3
                inner, aa, bb = total[r : r + 1], total[r + 1 : r + 2], total[r + 2 : r + 3]
                coef_a = 1.0 - inner / (2.0 * (aa + epsilon))
                coef_b = 1.0 - inner / (2.0 * (bb + epsilon))

                def mix(t, _, i=i, e=e, half=half, coef_a=coef_a, coef_b=coef_b):
                    span = pl.ds(pl.multiple_of(t * tile, tile), tile)
                    a = vec[i, e, span, :].astype(f32)
                    b = vec[i + half, e, span, :].astype(f32)
                    merged = (coef_a * a + coef_b * b).astype(bf16)
                    if half > 1:
                        vec[i, e, span, :] = merged
                    else:
                        new = w_ref[e, span, :].astype(f32) - learn_rate * merged.astype(f32)
                        nw_ref[e, span, :] = new.astype(bf16)
                    return 0

                lax.fori_loop(0, ff // tile, mix, 0)
        for copy in copies:
            copy.wait_send()
        half //= 2
        level += 1

    for copy in p_copies:
        copy.wait_recv()
    for b in range(blocks):
        total = folded(0, b)
        for k in range(1, n):
            total = total + inp[k - 1, pl.ds(b * block, block), :].astype(f32)
        gh_ref[pl.ds(b * block, block), :] = total.astype(bf16)

    for k in order:
        z_copies[k].wait_send()
    for k in range(1, n):
        h_copies[k - 1].wait_send()
        p_copies[k - 1].wait_send()
        pltpu.make_async_remote_copy(
            src_ref=part.at[k],
            dst_ref=part.at[k],
            send_sem=m_send.at[k - 1],
            recv_sem=m_recv.at[k - 1],
            device_id={"dp": near(k)},
            device_id_type=MESH,
        ).wait_send()


def per_device(hidden_rows, grad_send, row_index, block_expert, block_count, down_weight):
    n_e, n = lax.axis_size("expert"), lax.axis_size("dp")
    _, rows, ff = hidden_rows.shape
    width = grad_send.shape[2]
    local, _, cols = down_weight.shape
    cap = rows // n_e
    levels = n.bit_length() - 1
    stat_rows = -(-(n // 2 * local * 3) // 8) * 8
    vmem = pl.BlockSpec(memory_space=pltpu.VMEM)
    smem = pl.BlockSpec(memory_space=pltpu.SMEM)
    dma = pltpu.SemaphoreType.DMA
    grad_hidden, new_weight = pl.pallas_call(
        functools.partial(kernel, n_e, n),
        out_shape=(
            jax.ShapeDtypeStruct((rows, ff), bf16),
            jax.ShapeDtypeStruct((local, ff, cols), bf16),
        ),
        in_specs=[pl.BlockSpec(memory_space=pl.ANY), vmem, vmem, smem, smem, vmem],
        out_specs=(vmem, vmem),
        scratch_shapes=[
            pltpu.VMEM((n_e, cap, width), bf16),
            pltpu.VMEM((n, n_e, cap, cols), bf16),
            pltpu.VMEM((rows, rows), bf16),
            pltpu.VMEM((n - 1, rows, ff), bf16),
            pltpu.VMEM((n - 1, rows, ff), bf16),
            pltpu.VMEM((n - 1, rows, ff), bf16),
            dict(
                slots=pltpu.VMEM((n, rows, cols), bf16),
                vec=pltpu.VMEM((n, local, ff, cols), bf16),
            ),
            pltpu.VMEM((levels, stat_rows, 128), f32),
            pltpu.VMEM((levels, n - 1, stat_rows, 128), f32),
            dma((n_e - 1,)),
            dma((n_e - 1,)),
            dma((n - 1,)),
            dma((n - 1,)),
            dma((n - 1,)),
            dma((n - 1,)),
            dma((n - 1,)),
            dma((n - 1,)),
            dma((levels, n - 1)),
            dma((levels, n - 1)),
            dma,
        ],
        compiler_params=pltpu.CompilerParams(
            collective_id=0, has_side_effects=True, vmem_limit_bytes=58 * 1024 * 1024
        ),
    )(
        grad_send[0],
        hidden_rows[0],
        row_index.reshape(rows, 1),
        block_expert[0],
        block_count[0],
        down_weight,
    )
    return grad_hidden[None], new_weight


def solution(mesh):
    in_specs = (
        P("dp", "expert", None),
        P("dp", "expert", None),
        P("expert", None),
        P("expert", None),
        P("expert", None),
        P("expert", None, "dp"),
    )
    out_specs = (P("dp", "expert", None), P("expert", None, "dp"))
    return jax.shard_map(
        per_device, mesh=mesh, in_specs=in_specs, out_specs=out_specs, check_vma=False
    )
```

```python
import functools

import jax
import jax.numpy as jnp
from jax import lax
from jax.experimental import pallas as pl
from jax.experimental.pallas import tpu as pltpu
from jax.sharding import PartitionSpec as P

learn_rate = 0.01
epsilon = 1e-06
MESH = pl.DeviceIdType.MESH
bf16 = jnp.bfloat16
f32 = jnp.float32


def kernel(
    n_e,
    n,
    grad_ref,
    hidden_ref,
    index_ref,
    expert_ref,
    count_ref,
    w_ref,
    gh_ref,
    nw_ref,
    arrived,
    part,
    pick,
    hall,
    out_a,
    out_b,
    in_a,
    in_b,
    next_a,
    next_b,
    last_a,
    last_b,
    own_sum,
    v,
    stat,
    stat_in,
    z_send,
    z_recv,
    m_send,
    m_recv,
    h_send,
    h_recv,
    d_send,
    d_recv,
    p_send,
    p_recv,
    q_send,
    q_recv,
    s_send,
    s_recv,
    own_sem,
):
    rows, ff = hidden_ref.shape
    cap = arrived.shape[1]
    local, _, cols = w_ref.shape
    blocks = expert_ref.shape[0]
    block = rows // blocks
    me_e, me = lax.axis_index("expert"), lax.axis_index("dp")

    def near_e(k):
        return lax.rem(me_e + k + n_e, n_e)

    n_b = 2 ** (n.bit_length() // 2)
    n_a = n // n_b
    me_a, me_b = lax.div(me, n_b), lax.rem(me, n_b)

    def near(k):
        return lax.rem(me_a + k // n_b, n_a) * n_b + lax.rem(me_b + k % n_b, n_b)

    def back(k):
        return lax.rem(me_a + n_a - k // n_b, n_a) * n_b + lax.rem(me_b + n_b - k % n_b, n_b)

    line_a = [d * n_b for d in range(1, n_a)]
    line_b = list(range(1, n_b))

    barrier = pltpu.get_barrier_semaphore()
    for k in range(1, n_e):
        pl.semaphore_signal(barrier, inc=1, device_id={"expert": near_e(k)}, device_id_type=MESH)
    for k in range(1, n):
        pl.semaphore_signal(barrier, inc=1, device_id={"dp": near(k)}, device_id_type=MESH)
    own = pltpu.make_async_copy(grad_ref.at[pl.ds(me_e * cap, cap)], arrived.at[me_e], own_sem)
    own.start()
    pl.semaphore_wait(barrier, n_e + n - 2)

    order = sorted(range(1, n_e), key=lambda k: -min(k, n_e - k))
    z_copies = {}
    for k in order:
        to = near_e(k)
        z_copies[k] = pltpu.make_async_remote_copy(
            src_ref=grad_ref.at[pl.ds(to * cap, cap)],
            dst_ref=arrived.at[me_e],
            send_sem=z_send.at[k - 1],
            recv_sem=z_recv.at[k - 1],
            device_id={"expert": to},
            device_id_type=MESH,
        )
        z_copies[k].start()
    h_copies = {}
    for k in line_a + line_b:
        h_copies[k] = pltpu.make_async_remote_copy(
            src_ref=hidden_ref,
            dst_ref=hall.at[k - 1],
            send_sem=h_send.at[k - 1],
            recv_sem=h_recv.at[k - 1],
            device_id={"dp": near(k)},
            device_id_type=MESH,
        )
        h_copies[k].start()
    d_copies = {}

    def relay(k, source, to, which):
        span = pl.ds(which * (rows // 2), rows // 2)
        copy = pltpu.make_async_remote_copy(
            src_ref=hall.at[source - 1, span],
            dst_ref=hall.at[k - 1, span],
            send_sem=d_send.at[k - 1, which],
            recv_sem=d_recv.at[k - 1, which],
            device_id={"dp": near(to)},
            device_id_type=MESH,
        )
        copy.start()
        d_copies[k, which] = copy

    received = lax.broadcasted_iota(jnp.int32, (rows, rows), 0)
    hits = jnp.where(index_ref[...] == received, 1.0, 0.0).astype(f32).T
    for b in range(blocks):
        slot = lax.broadcasted_iota(jnp.int32, (block, rows), 0)
        live = jnp.where(slot < count_ref[b], hits[b * block : (b + 1) * block], 0.0)
        pick[pl.ds(b * block, block), :] = live.astype(bf16)

    def forward(source):
        for k in range(1, n):
            to = near(k)
            pltpu.make_async_remote_copy(
                src_ref=arrived.at[source, :, pl.ds(pl.multiple_of(to * cols, cols), cols)],
                dst_ref=part.at[k, source],
                send_sem=m_send.at[k - 1],
                recv_sem=m_recv.at[k - 1],
                device_id={"dp": to},
                device_id_type=MESH,
            ).start()

    own.wait()
    forward(me_e)
    for turn, k in enumerate([1] + [k for k in order if k != 1]):
        z_copies[k].wait_recv()
        forward(near_e(-k))
        if turn == n_e // 2 - 1:
            for k_a in line_a:
                h_copies[k_a].wait_recv()
                for k_b in line_b:
                    relay(k_a + k_b, k_a, k_b, 0)
            for k_b in line_b:
                h_copies[k_b].wait_recv()
                for k_a in line_a:
                    relay(k_a + k_b, k_b, k_a, 1)

    def slots(k):
        flat = part[k].reshape(rows, cols)
        return jnp.dot(pick[...], flat, preferred_element_type=f32).astype(bf16)

    def folded(k, b):
        return lax.dot_general(
            part_slots[k, pl.ds(b * block, block), :],
            w_ref[expert_ref[b]],
            (((1,), (1,)), ((), ())),
            preferred_element_type=f32,
        )

    part_slots = v["slots"]
    vec = v["vec"]

    p_copies = []
    half_ff = ff // 2

    def send(src, dst, sems, side, d, to):
        copy = pltpu.make_async_remote_copy(
            src_ref=src,
            dst_ref=dst,
            send_sem=sems[0].at[side, d],
            recv_sem=sems[1].at[side, d],
            device_id={"dp": to},
            device_id_type=MESH,
        )
        copy.start()
        p_copies.append(copy)
        return copy

    first, second = (p_send, p_recv), (q_send, q_recv)
    stage_a, stage_b = [], []
    made = set()
    for k in list(range(n - 1, 0, -1)) + [0]:
        if k:
            pltpu.make_async_remote_copy(
                src_ref=part.at[k],
                dst_ref=part.at[k],
                send_sem=m_send.at[k - 1],
                recv_sem=m_recv.at[k - 1],
                device_id={"dp": near(k)},
                device_id_type=MESH,
            ).wait_recv()
        else:
            for s in range(n_e):
                part[0, s] = arrived[s, :, pl.ds(pl.multiple_of(me * cols, cols), cols)]
        part_slots[k] = slots(k)
        d_a, d_b = k // n_b, k % n_b
        for b in range(blocks):
            span = pl.ds(b * block, block)
            value = folded(k, b)
            if k:
                out_a[k, span, :] = value[:, :half_ff].astype(bf16)
                out_b[d_b * n_a + d_a, span, :] = value[:, half_ff:].astype(bf16)
            else:
                own_sum[span, :] = value
        made.add(k)
        if d_a and all(d_a * n_b + d in made for d in range(n_b)):
            stage_a.append(
                send(
                    out_a.at[pl.ds(d_a * n_b, n_b)],
                    in_a.at[d_a - 1],
                    first,
                    0,
                    d_a - 1,
                    back(d_a * n_b),
                )
            )
        if d_b and all(d * n_b + d_b in made for d in range(n_a)):
            stage_b.append(
                send(
                    out_b.at[pl.ds(d_b * n_a, n_a)],
                    in_b.at[d_b - 1],
                    first,
                    1,
                    d_b - 1,
                    back(d_b),
                )
            )

    def gradient(k, hidden):
        for e in range(local):
            pieces = [
                jnp.where(expert_ref[b] == e, hidden[pl.ds(b * block, block), :], jnp.zeros((), bf16))
                for b in range(blocks)
            ]
            chosen = jnp.concatenate(pieces, axis=0)
            vec[back(k), e] = lax.dot_general(
                chosen, part_slots[k], (((0,), (0,)), ((), ())), preferred_element_type=f32
            ).astype(bf16)

    gradient(0, hidden_ref)
    for k in line_a + line_b:
        gradient(k, hall.at[k - 1])
    for k_a in line_a:
        for k_b in line_b:
            for which in range(2):
                d_copies[k_a + k_b, which].wait_recv()
            gradient(k_a + k_b, hall.at[k_a + k_b - 1])

    for copy in stage_a + stage_b:
        copy.wait_recv()
    p_last = []
    for d in range(1, n_b):
        for b in range(blocks):
            span = pl.ds(b * block, block)
            total = out_a[d, span, :].astype(f32)
            for g in range(n_a - 1):
                total = total + in_a[g, d, span, :].astype(f32)
            next_a[d - 1, span, :] = total.astype(bf16)
        p_last.append(send(next_a.at[d - 1], last_a.at[d - 1], second, 0, d - 1, back(d)))
    for d in range(1, n_a):
        for b in range(blocks):
            span = pl.ds(b * block, block)
            total = out_b[d, span, :].astype(f32)
            for g in range(n_b - 1):
                total = total + in_b[g, d, span, :].astype(f32)
            next_b[d - 1, span, :] = total.astype(bf16)
        p_last.append(send(next_b.at[d - 1], last_b.at[d - 1], second, 1, d - 1, back(d * n_b)))

    tile = 64
    half = n // 2
    level = 0
    while half >= 1:
        count = half * local * 3
        for i in range(half):
            for e in range(local):

                def body(t, sums, i=i, e=e, half=half):
                    span = pl.ds(pl.multiple_of(t * tile, tile), tile)
                    a = vec[i, e, span, :].astype(f32)
                    b = vec[i + half, e, span, :].astype(f32)
                    return tuple(
                        total + jnp.sum(x.reshape(tile // 8, 8, cols), axis=0)
                        for total, x in zip(sums, (a * b, a * a, b * b))
                    )

                zero = jnp.zeros((8, cols), f32)
                sums = lax.fori_loop(0, ff // tile, body, (zero, zero, zero))
                for m in range(3):
                    narrow = sums[m][:, :128]
                    for c in range(1, cols // 128):
                        narrow = narrow + sums[m][:, c * 128 : (c + 1) * 128]
                    r = (i * local + e) * 3 + m
                    stat[level, pl.ds(r, 1), :] = jnp.sum(narrow, axis=0, keepdims=True)
        copies = []
        for k in range(1, n):
            copy = pltpu.make_async_remote_copy(
                src_ref=stat.at[level],
                dst_ref=stat_in.at[level, k - 1],
                send_sem=s_send.at[level, k - 1],
                recv_sem=s_recv.at[level, k - 1],
                device_id={"dp": near(k)},
                device_id_type=MESH,
            )
            copy.start()
            copies.append(copy)
        for copy in copies:
            copy.wait_recv()
        total = stat[level, :count, :]
        for k in range(1, n):
            total = total + stat_in[level, k - 1, :count, :]
        total = jnp.sum(total, axis=1, keepdims=True)
        for i in range(half):
            for e in range(local):
                r = (i * local + e) * 3
                inner, aa, bb = total[r : r + 1], total[r + 1 : r + 2], total[r + 2 : r + 3]
                coef_a = 1.0 - inner / (2.0 * (aa + epsilon))
                coef_b = 1.0 - inner / (2.0 * (bb + epsilon))

                def mix(t, _, i=i, e=e, half=half, coef_a=coef_a, coef_b=coef_b):
                    span = pl.ds(pl.multiple_of(t * tile, tile), tile)
                    a = vec[i, e, span, :].astype(f32)
                    b = vec[i + half, e, span, :].astype(f32)
                    merged = (coef_a * a + coef_b * b).astype(bf16)
                    if half > 1:
                        vec[i, e, span, :] = merged
                    else:
                        new = w_ref[e, span, :].astype(f32) - learn_rate * merged.astype(f32)
                        nw_ref[e, span, :] = new.astype(bf16)
                    return 0

                lax.fori_loop(0, ff // tile, mix, 0)
        for copy in copies:
            copy.wait_send()
        half //= 2
        level += 1

    for copy in p_last:
        copy.wait_recv()
    for b in range(blocks):
        span = pl.ds(b * block, block)
        total = own_sum[span, :half_ff]
        for g in range(n_a - 1):
            total = total + in_a[g, 0, span, :].astype(f32)
        for g in range(n_b - 1):
            total = total + last_a[g, span, :].astype(f32)
        gh_ref[span, :half_ff] = total.astype(bf16)
        total = own_sum[span, half_ff:]
        for g in range(n_b - 1):
            total = total + in_b[g, 0, span, :].astype(f32)
        for g in range(n_a - 1):
            total = total + last_b[g, span, :].astype(f32)
        gh_ref[span, half_ff:] = total.astype(bf16)

    for k in order:
        z_copies[k].wait_send()
    for copy in list(h_copies.values()) + list(d_copies.values()) + p_copies:
        copy.wait_send()
    for k in range(1, n):
        pltpu.make_async_remote_copy(
            src_ref=part.at[k],
            dst_ref=part.at[k],
            send_sem=m_send.at[k - 1],
            recv_sem=m_recv.at[k - 1],
            device_id={"dp": near(k)},
            device_id_type=MESH,
        ).wait_send()


def per_device(hidden_rows, grad_send, row_index, block_expert, block_count, down_weight):
    n_e, n = lax.axis_size("expert"), lax.axis_size("dp")
    _, rows, ff = hidden_rows.shape
    width = grad_send.shape[2]
    local, _, cols = down_weight.shape
    cap = rows // n_e
    levels = n.bit_length() - 1
    n_b = 2 ** (n.bit_length() // 2)
    n_a = n // n_b
    stat_rows = -(-(n // 2 * local * 3) // 8) * 8
    vmem = pl.BlockSpec(memory_space=pltpu.VMEM)
    smem = pl.BlockSpec(memory_space=pltpu.SMEM)
    dma = pltpu.SemaphoreType.DMA
    grad_hidden, new_weight = pl.pallas_call(
        functools.partial(kernel, n_e, n),
        out_shape=(
            jax.ShapeDtypeStruct((rows, ff), bf16),
            jax.ShapeDtypeStruct((local, ff, cols), bf16),
        ),
        in_specs=[pl.BlockSpec(memory_space=pl.ANY), vmem, vmem, smem, smem, vmem],
        out_specs=(vmem, vmem),
        scratch_shapes=[
            pltpu.VMEM((n_e, cap, width), bf16),
            pltpu.VMEM((n, n_e, cap, cols), bf16),
            pltpu.VMEM((rows, rows), bf16),
            pltpu.VMEM((n - 1, rows, ff), bf16),
            pltpu.VMEM((n, rows, ff // 2), bf16),
            pltpu.VMEM((n, rows, ff // 2), bf16),
            pltpu.VMEM((n_a - 1, n_b, rows, ff // 2), bf16),
            pltpu.VMEM((n_b - 1, n_a, rows, ff // 2), bf16),
            pltpu.VMEM((n_b - 1, rows, ff // 2), bf16),
            pltpu.VMEM((n_a - 1, rows, ff // 2), bf16),
            pltpu.VMEM((n_b - 1, rows, ff // 2), bf16),
            pltpu.VMEM((n_a - 1, rows, ff // 2), bf16),
            pltpu.VMEM((rows, ff), f32),
            dict(
                slots=pltpu.VMEM((n, rows, cols), bf16),
                vec=pltpu.VMEM((n, local, ff, cols), bf16),
            ),
            pltpu.VMEM((levels, stat_rows, 128), f32),
            pltpu.VMEM((levels, n - 1, stat_rows, 128), f32),
            dma((n_e - 1,)),
            dma((n_e - 1,)),
            dma((n - 1,)),
            dma((n - 1,)),
            dma((n - 1,)),
            dma((n - 1,)),
            dma((n - 1, 2)),
            dma((n - 1, 2)),
            dma((2, max(n_a, n_b) - 1)),
            dma((2, max(n_a, n_b) - 1)),
            dma((2, max(n_a, n_b) - 1)),
            dma((2, max(n_a, n_b) - 1)),
            dma((levels, n - 1)),
            dma((levels, n - 1)),
            dma,
        ],
        compiler_params=pltpu.CompilerParams(
            collective_id=0, has_side_effects=True, vmem_limit_bytes=58 * 1024 * 1024
        ),
    )(
        grad_send[0],
        hidden_rows[0],
        row_index,
        block_expert[0],
        block_count[0],
        down_weight,
    )
    return grad_hidden[None], new_weight


def solution(mesh):
    in_specs = (
        P("dp", "expert", None),
        P("dp", "expert", None),
        P("expert", None),
        P("expert", None),
        P("expert", None),
        P("expert", None, "dp"),
    )
    out_specs = (P("dp", "expert", None), P("expert", None, "dp"))
    return jax.shard_map(
        per_device, mesh=mesh, in_specs=in_specs, out_specs=out_specs, check_vma=False
    )
```

```python
import functools

import jax
import jax.numpy as jnp
from jax import lax
from jax.experimental import pallas as pl
from jax.experimental.pallas import tpu as pltpu
from jax.sharding import PartitionSpec as P

learn_rate = 0.01
epsilon = 1e-06
MESH = pl.DeviceIdType.MESH
bf16 = jnp.bfloat16
f32 = jnp.float32


def kernel(
    n_e,
    n,
    grad_ref,
    hidden_ref,
    index_ref,
    expert_ref,
    count_ref,
    w_ref,
    gh_ref,
    nw_ref,
    stage,
    part,
    pick,
    hall,
    out_a,
    out_b,
    in_a,
    in_b,
    next_a,
    next_b,
    last_a,
    last_b,
    own_sum,
    v,
    stat,
    stat_in,
    z_send,
    z_recv,
    m_send,
    m_recv,
    h_send,
    h_recv,
    d_send,
    d_recv,
    p_send,
    p_recv,
    q_send,
    q_recv,
    s_send,
    s_recv,
    own_sem,
):
    rows, ff = hidden_ref.shape
    cap = part.shape[2]
    local, _, cols = w_ref.shape
    blocks = expert_ref.shape[0]
    block = rows // blocks
    me_e, me = lax.axis_index("expert"), lax.axis_index("dp")

    def near_e(k):
        return lax.rem(me_e + k + n_e, n_e)

    n_b = 2 ** (n.bit_length() // 2)
    n_a = n // n_b
    me_a, me_b = lax.div(me, n_b), lax.rem(me, n_b)

    def near(k):
        return lax.rem(me_a + k // n_b, n_a) * n_b + lax.rem(me_b + k % n_b, n_b)

    def back(k):
        return lax.rem(me_a + n_a - k // n_b, n_a) * n_b + lax.rem(me_b + n_b - k % n_b, n_b)

    line_a = [d * n_b for d in range(1, n_a)]
    line_b = list(range(1, n_b))

    barrier = pltpu.get_barrier_semaphore()
    for k in range(1, n_e):
        pl.semaphore_signal(barrier, inc=1, device_id={"expert": near_e(k)}, device_id_type=MESH)
    for k in range(1, n):
        pl.semaphore_signal(barrier, inc=1, device_id={"dp": near(k)}, device_id_type=MESH)
    mine = pl.ds(pl.multiple_of(me * cols, cols), cols)
    own = pltpu.make_async_copy(grad_ref.at[me_e, :, mine], part.at[0, me_e], own_sem)
    own.start()
    pl.semaphore_wait(barrier, n_e + n - 2)

    m_copies = {}
    for k in line_a + line_b + [a + b for a in line_a for b in line_b]:
        to = near(k)
        m_copies[k] = pltpu.make_async_remote_copy(
            src_ref=grad_ref.at[:, :, pl.ds(pl.multiple_of(to * cols, cols), cols)],
            dst_ref=stage.at[k - 1],
            send_sem=m_send.at[k - 1],
            recv_sem=m_recv.at[k - 1],
            device_id={"dp": to},
            device_id_type=MESH,
        )
        m_copies[k].start()

    order = sorted(range(1, n_e), key=lambda k: -min(k, n_e - k))

    def spread(k):
        for j in order:
            to = near_e(j)
            pltpu.make_async_remote_copy(
                src_ref=stage.at[k - 1, to] if k else grad_ref.at[to, :, mine],
                dst_ref=part.at[k, me_e],
                send_sem=z_send.at[k],
                recv_sem=z_recv.at[k],
                device_id={"expert": to},
                device_id_type=MESH,
            ).start()

    def spread_all(k):
        others = part.at[k, pl.ds(0, n_e - 1)]
        return pltpu.make_async_remote_copy(
            src_ref=others,
            dst_ref=others,
            send_sem=z_send.at[k],
            recv_sem=z_recv.at[k],
            device_id={"expert": near_e(1)},
            device_id_type=MESH,
        )

    spread(0)
    h_copies = {}
    for k in line_a + line_b:
        h_copies[k] = pltpu.make_async_remote_copy(
            src_ref=hidden_ref,
            dst_ref=hall.at[k - 1],
            send_sem=h_send.at[k - 1],
            recv_sem=h_recv.at[k - 1],
            device_id={"dp": near(k)},
            device_id_type=MESH,
        )
    d_copies = {}

    def relay(k, source, to, which):
        span = pl.ds(which * (rows // 2), rows // 2)
        copy = pltpu.make_async_remote_copy(
            src_ref=hall.at[source - 1, span],
            dst_ref=hall.at[k - 1, span],
            send_sem=d_send.at[k - 1, which],
            recv_sem=d_recv.at[k - 1, which],
            device_id={"dp": near(to)},
            device_id_type=MESH,
        )
        copy.start()
        d_copies[k, which] = copy

    received = lax.broadcasted_iota(jnp.int32, (rows, rows), 0)
    hits = jnp.where(index_ref[...] == received, 1.0, 0.0).astype(f32).T
    for b in range(blocks):
        slot = lax.broadcasted_iota(jnp.int32, (block, rows), 0)
        live = jnp.where(slot < count_ref[b], hits[b * block : (b + 1) * block], 0.0)
        pick[pl.ds(b * block, block), :] = live.astype(bf16)

    for k in m_copies:
        m_copies[k].wait_recv()
        spread(k)
        part[k, me_e] = stage[k - 1, me_e]
    for k in h_copies:
        h_copies[k].start()
    own.wait()

    def relay_all():
        for k_a in line_a:
            h_copies[k_a].wait_recv()
            for k_b in line_b:
                relay(k_a + k_b, k_a, k_b, 0)
        for k_b in line_b:
            h_copies[k_b].wait_recv()
            for k_a in line_a:
                relay(k_a + k_b, k_b, k_a, 1)

    def slots(k):
        flat = part[k].reshape(rows, cols)
        return jnp.dot(pick[...], flat, preferred_element_type=f32).astype(bf16)

    def folded(k, b):
        return lax.dot_general(
            part_slots[k, pl.ds(b * block, block), :],
            w_ref[expert_ref[b]],
            (((1,), (1,)), ((), ())),
            preferred_element_type=f32,
        )

    part_slots = v["slots"]
    vec = v["vec"]

    p_copies = []
    half_ff = ff // 2

    def send(src, dst, sems, side, d, to):
        copy = pltpu.make_async_remote_copy(
            src_ref=src,
            dst_ref=dst,
            send_sem=sems[0].at[side, d],
            recv_sem=sems[1].at[side, d],
            device_id={"dp": to},
            device_id_type=MESH,
        )
        copy.start()
        p_copies.append(copy)
        return copy

    first, second = (p_send, p_recv), (q_send, q_recv)
    p_first = []
    for turn, k in enumerate([0] + list(m_copies)):
        if turn == n - 1:
            relay_all()
        spread_all(k).wait_recv()
        part_slots[k] = slots(k)
        d_a, d_b = k // n_b, k % n_b
        for b in range(blocks):
            span = pl.ds(b * block, block)
            value = folded(k, b)
            if k:
                out_a[k, span, :] = value[:, :half_ff].astype(bf16)
                out_b[d_b * n_a + d_a, span, :] = value[:, half_ff:].astype(bf16)
            else:
                own_sum[span, :] = value
        if d_a:
            to = back(d_a * n_b)
            p_first.append(send(out_a.at[k], in_a.at[d_a - 1, d_b], first, 0, k, to))
        if d_b:
            source = out_b.at[d_b * n_a + d_a]
            p_first.append(send(source, in_b.at[d_b - 1, d_a], first, 1, k, back(d_b)))

    def gradient(k, hidden):
        for e in range(local):
            pieces = [
                jnp.where(expert_ref[b] == e, hidden[pl.ds(b * block, block), :], jnp.zeros((), bf16))
                for b in range(blocks)
            ]
            chosen = jnp.concatenate(pieces, axis=0)
            vec[back(k), e] = lax.dot_general(
                chosen, part_slots[k], (((0,), (0,)), ((), ())), preferred_element_type=f32
            ).astype(bf16)

    gradient(0, hidden_ref)
    for k in line_a + line_b:
        gradient(k, hall.at[k - 1])
    for k_a in line_a:
        for k_b in line_b:
            for which in range(2):
                d_copies[k_a + k_b, which].wait_recv()
            gradient(k_a + k_b, hall.at[k_a + k_b - 1])

    for copy in p_first:
        copy.wait_recv()
    p_last = []
    for d in range(1, n_b):
        for b in range(blocks):
            span = pl.ds(b * block, block)
            total = out_a[d, span, :].astype(f32)
            for g in range(n_a - 1):
                total = total + in_a[g, d, span, :].astype(f32)
            next_a[d - 1, span, :] = total.astype(bf16)
        p_last.append(send(next_a.at[d - 1], last_a.at[d - 1], second, 0, d - 1, back(d)))
    for d in range(1, n_a):
        for b in range(blocks):
            span = pl.ds(b * block, block)
            total = out_b[d, span, :].astype(f32)
            for g in range(n_b - 1):
                total = total + in_b[g, d, span, :].astype(f32)
            next_b[d - 1, span, :] = total.astype(bf16)
        p_last.append(send(next_b.at[d - 1], last_b.at[d - 1], second, 1, d - 1, back(d * n_b)))

    tile = 64
    half = n // 2
    level = 0
    while half >= 1:
        count = half * local * 3
        for i in range(half):
            for e in range(local):

                def body(t, sums, i=i, e=e, half=half):
                    span = pl.ds(pl.multiple_of(t * tile, tile), tile)
                    a = vec[i, e, span, :].astype(f32)
                    b = vec[i + half, e, span, :].astype(f32)
                    return tuple(
                        total + jnp.sum(x.reshape(tile // 8, 8, cols), axis=0)
                        for total, x in zip(sums, (a * b, a * a, b * b))
                    )

                zero = jnp.zeros((8, cols), f32)
                sums = lax.fori_loop(0, ff // tile, body, (zero, zero, zero))
                for m in range(3):
                    narrow = sums[m][:, :128]
                    for c in range(1, cols // 128):
                        narrow = narrow + sums[m][:, c * 128 : (c + 1) * 128]
                    r = (i * local + e) * 3 + m
                    stat[level, pl.ds(r, 1), :] = jnp.sum(narrow, axis=0, keepdims=True)
        copies = []
        for k in range(1, n):
            copy = pltpu.make_async_remote_copy(
                src_ref=stat.at[level],
                dst_ref=stat_in.at[level, k - 1],
                send_sem=s_send.at[level, k - 1],
                recv_sem=s_recv.at[level, k - 1],
                device_id={"dp": near(k)},
                device_id_type=MESH,
            )
            copy.start()
            copies.append(copy)
        for copy in copies:
            copy.wait_recv()
        total = stat[level, :count, :]
        for k in range(1, n):
            total = total + stat_in[level, k - 1, :count, :]
        total = jnp.sum(total, axis=1, keepdims=True)
        for i in range(half):
            for e in range(local):
                r = (i * local + e) * 3
                inner, aa, bb = total[r : r + 1], total[r + 1 : r + 2], total[r + 2 : r + 3]
                coef_a = 1.0 - inner / (2.0 * (aa + epsilon))
                coef_b = 1.0 - inner / (2.0 * (bb + epsilon))

                def mix(t, _, i=i, e=e, half=half, coef_a=coef_a, coef_b=coef_b):
                    span = pl.ds(pl.multiple_of(t * tile, tile), tile)
                    a = vec[i, e, span, :].astype(f32)
                    b = vec[i + half, e, span, :].astype(f32)
                    merged = (coef_a * a + coef_b * b).astype(bf16)
                    if half > 1:
                        vec[i, e, span, :] = merged
                    else:
                        new = w_ref[e, span, :].astype(f32) - learn_rate * merged.astype(f32)
                        nw_ref[e, span, :] = new.astype(bf16)
                    return 0

                lax.fori_loop(0, ff // tile, mix, 0)
        for copy in copies:
            copy.wait_send()
        half //= 2
        level += 1

    for copy in p_last:
        copy.wait_recv()
    for b in range(blocks):
        span = pl.ds(b * block, block)
        total = own_sum[span, :half_ff]
        for g in range(n_a - 1):
            total = total + in_a[g, 0, span, :].astype(f32)
        for g in range(n_b - 1):
            total = total + last_a[g, span, :].astype(f32)
        gh_ref[span, :half_ff] = total.astype(bf16)
        total = own_sum[span, half_ff:]
        for g in range(n_b - 1):
            total = total + in_b[g, 0, span, :].astype(f32)
        for g in range(n_a - 1):
            total = total + last_b[g, span, :].astype(f32)
        gh_ref[span, half_ff:] = total.astype(bf16)

    for k in range(n):
        spread_all(k).wait_send()
    for group in (m_copies, h_copies, d_copies):
        for copy in group.values():
            copy.wait_send()
    for copy in p_copies:
        copy.wait_send()


def per_device(hidden_rows, grad_send, row_index, block_expert, block_count, down_weight):
    n_e, n = lax.axis_size("expert"), lax.axis_size("dp")
    _, rows, ff = hidden_rows.shape
    width = grad_send.shape[2]
    local, _, cols = down_weight.shape
    cap = rows // n_e
    levels = n.bit_length() - 1
    n_b = 2 ** (n.bit_length() // 2)
    n_a = n // n_b
    stat_rows = -(-(n // 2 * local * 3) // 8) * 8
    vmem = pl.BlockSpec(memory_space=pltpu.VMEM)
    smem = pl.BlockSpec(memory_space=pltpu.SMEM)
    dma = pltpu.SemaphoreType.DMA
    grad_hidden, new_weight = pl.pallas_call(
        functools.partial(kernel, n_e, n),
        out_shape=(
            jax.ShapeDtypeStruct((rows, ff), bf16),
            jax.ShapeDtypeStruct((local, ff, cols), bf16),
        ),
        in_specs=[pl.BlockSpec(memory_space=pl.ANY), vmem, vmem, smem, smem, vmem],
        out_specs=(vmem, vmem),
        scratch_shapes=[
            pltpu.VMEM((n - 1, n_e, cap, cols), bf16),
            pltpu.VMEM((n, n_e, cap, cols), bf16),
            pltpu.VMEM((rows, rows), bf16),
            pltpu.VMEM((n - 1, rows, ff), bf16),
            pltpu.VMEM((n, rows, ff // 2), bf16),
            pltpu.VMEM((n, rows, ff // 2), bf16),
            pltpu.VMEM((n_a - 1, n_b, rows, ff // 2), bf16),
            pltpu.VMEM((n_b - 1, n_a, rows, ff // 2), bf16),
            pltpu.VMEM((n_b - 1, rows, ff // 2), bf16),
            pltpu.VMEM((n_a - 1, rows, ff // 2), bf16),
            pltpu.VMEM((n_b - 1, rows, ff // 2), bf16),
            pltpu.VMEM((n_a - 1, rows, ff // 2), bf16),
            pltpu.VMEM((rows, ff), f32),
            dict(
                slots=pltpu.VMEM((n, rows, cols), bf16),
                vec=pltpu.VMEM((n, local, ff, cols), bf16),
            ),
            pltpu.VMEM((levels, stat_rows, 128), f32),
            pltpu.VMEM((levels, n - 1, stat_rows, 128), f32),
            dma((n,)),
            dma((n,)),
            dma((n - 1,)),
            dma((n - 1,)),
            dma((n - 1,)),
            dma((n - 1,)),
            dma((n - 1, 2)),
            dma((n - 1, 2)),
            dma((2, n)),
            dma((2, n)),
            dma((2, max(n_a, n_b) - 1)),
            dma((2, max(n_a, n_b) - 1)),
            dma((levels, n - 1)),
            dma((levels, n - 1)),
            dma,
        ],
        compiler_params=pltpu.CompilerParams(
            collective_id=0, has_side_effects=True, vmem_limit_bytes=58 * 1024 * 1024
        ),
    )(
        grad_send.reshape(n_e, cap, width),
        hidden_rows[0],
        row_index,
        block_expert[0],
        block_count[0],
        down_weight,
    )
    return grad_hidden[None], new_weight


def solution(mesh):
    in_specs = (
        P("dp", "expert", None),
        P("dp", "expert", None),
        P("expert", None),
        P("expert", None),
        P("expert", None),
        P("expert", None, "dp"),
    )
    out_specs = (P("dp", "expert", None), P("expert", None, "dp"))
    return jax.shard_map(
        per_device, mesh=mesh, in_specs=in_specs, out_specs=out_specs, check_vma=False
    )
```

```python
import functools

import jax
import jax.numpy as jnp
from jax import lax
from jax.experimental import pallas as pl
from jax.experimental.pallas import tpu as pltpu
from jax.sharding import PartitionSpec as P

learn_rate = 0.01
epsilon = 1e-06
MESH = pl.DeviceIdType.MESH
bf16 = jnp.bfloat16
f32 = jnp.float32


def kernel(
    n_e,
    n,
    grad_ref,
    hidden_ref,
    index_ref,
    expert_ref,
    count_ref,
    w_ref,
    gh_ref,
    nw_ref,
    stage,
    part,
    pick,
    hall,
    out_a,
    out_b,
    in_a,
    in_b,
    next_a,
    next_b,
    last_a,
    last_b,
    own_sum,
    v,
    stat,
    stat_in,
    z_send,
    z_recv,
    m_send,
    m_recv,
    h_send,
    h_recv,
    d_send,
    d_recv,
    p_send,
    p_recv,
    q_send,
    q_recv,
    s_send,
    s_recv,
    own_sem,
):
    rows, ff = hidden_ref.shape
    cap = part.shape[2]
    local, _, cols = w_ref.shape
    blocks = expert_ref.shape[0]
    block = rows // blocks
    me_e, me = lax.axis_index("expert"), lax.axis_index("dp")

    def near_e(k):
        return lax.rem(me_e + k + n_e, n_e)

    n_b = 2 ** (n.bit_length() // 2)
    n_a = n // n_b
    me_a, me_b = lax.div(me, n_b), lax.rem(me, n_b)

    def near(k):
        return lax.rem(me_a + k // n_b, n_a) * n_b + lax.rem(me_b + k % n_b, n_b)

    def back(k):
        return lax.rem(me_a + n_a - k // n_b, n_a) * n_b + lax.rem(me_b + n_b - k % n_b, n_b)

    line_a = [d * n_b for d in range(1, n_a)]
    line_b = list(range(1, n_b))

    barrier = pltpu.get_barrier_semaphore()
    for k in range(1, n_e):
        pl.semaphore_signal(barrier, inc=1, device_id={"expert": near_e(k)}, device_id_type=MESH)
    for k in range(1, n):
        pl.semaphore_signal(barrier, inc=1, device_id={"dp": near(k)}, device_id_type=MESH)
    mine = pl.ds(pl.multiple_of(me * cols, cols), cols)
    own = pltpu.make_async_copy(grad_ref.at[me_e, :, mine], part.at[0, me_e], own_sem)
    own.start()
    pl.semaphore_wait(barrier, n_e + n - 2)

    m_copies = {}
    for k in line_a + line_b + [a + b for a in line_a for b in line_b]:
        to = near(k)
        m_copies[k] = pltpu.make_async_remote_copy(
            src_ref=grad_ref.at[:, :, pl.ds(pl.multiple_of(to * cols, cols), cols)],
            dst_ref=stage.at[k - 1],
            send_sem=m_send.at[k - 1],
            recv_sem=m_recv.at[k - 1],
            device_id={"dp": to},
            device_id_type=MESH,
        )
        m_copies[k].start()

    order = sorted(range(1, n_e), key=lambda k: -min(k, n_e - k))

    def spread(k):
        for j in order:
            to = near_e(j)
            pltpu.make_async_remote_copy(
                src_ref=stage.at[k - 1, to] if k else grad_ref.at[to, :, mine],
                dst_ref=part.at[k, me_e],
                send_sem=z_send.at[k],
                recv_sem=z_recv.at[k],
                device_id={"expert": to},
                device_id_type=MESH,
            ).start()

    def spread_all(k):
        others = part.at[k, pl.ds(0, n_e - 1)]
        return pltpu.make_async_remote_copy(
            src_ref=others,
            dst_ref=others,
            send_sem=z_send.at[k],
            recv_sem=z_recv.at[k],
            device_id={"expert": near_e(1)},
            device_id_type=MESH,
        )

    spread(0)
    h_copies = {}
    for k in line_a + line_b:
        h_copies[k] = pltpu.make_async_remote_copy(
            src_ref=hidden_ref,
            dst_ref=hall.at[k - 1],
            send_sem=h_send.at[k - 1],
            recv_sem=h_recv.at[k - 1],
            device_id={"dp": near(k)},
            device_id_type=MESH,
        )
    d_copies = {}

    def relay(k, source, to, which):
        span = pl.ds(which * (rows // 2), rows // 2)
        copy = pltpu.make_async_remote_copy(
            src_ref=hall.at[source - 1, span],
            dst_ref=hall.at[k - 1, span],
            send_sem=d_send.at[k - 1, which],
            recv_sem=d_recv.at[k - 1, which],
            device_id={"dp": near(to)},
            device_id_type=MESH,
        )
        copy.start()
        d_copies[k, which] = copy

    received = lax.broadcasted_iota(jnp.int32, (rows, rows), 0)
    hits = jnp.where(index_ref[...] == received, 1.0, 0.0).astype(f32).T
    for b in range(blocks):
        slot = lax.broadcasted_iota(jnp.int32, (block, rows), 0)
        live = jnp.where(slot < count_ref[b], hits[b * block : (b + 1) * block], 0.0)
        pick[pl.ds(b * block, block), :] = live.astype(bf16)

    for k in m_copies:
        m_copies[k].wait_recv()
        spread(k)
        part[k, me_e] = stage[k - 1, me_e]
    for k in h_copies:
        h_copies[k].start()
    own.wait()

    def relay_all():
        for k_a in line_a:
            h_copies[k_a].wait_recv()
            for k_b in line_b:
                relay(k_a + k_b, k_a, k_b, 0)
        for k_b in line_b:
            h_copies[k_b].wait_recv()
            for k_a in line_a:
                relay(k_a + k_b, k_b, k_a, 1)

    def slots(k):
        flat = part[k].reshape(rows, cols)
        return jnp.dot(pick[...], flat, preferred_element_type=f32).astype(bf16)

    def folded(k, b):
        return lax.dot_general(
            part_slots[k, pl.ds(b * block, block), :],
            w_ref[expert_ref[b]],
            (((1,), (1,)), ((), ())),
            preferred_element_type=f32,
        )

    part_slots = v["slots"]
    vec = v["vec"]

    p_copies = []
    half_ff = ff // 2

    def send(src, dst, sems, side, d, to):
        copy = pltpu.make_async_remote_copy(
            src_ref=src,
            dst_ref=dst,
            send_sem=sems[0].at[side, d],
            recv_sem=sems[1].at[side, d],
            device_id={"dp": to},
            device_id_type=MESH,
        )
        copy.start()
        p_copies.append(copy)
        return copy

    first, second = (p_send, p_recv), (q_send, q_recv)
    def gradient(k, hidden):
        for e in range(local):
            pieces = [
                jnp.where(expert_ref[b] == e, hidden[pl.ds(b * block, block), :], jnp.zeros((), bf16))
                for b in range(blocks)
            ]
            chosen = jnp.concatenate(pieces, axis=0)
            vec[back(k), e] = lax.dot_general(
                chosen, part_slots[k], (((0,), (0,)), ((), ())), preferred_element_type=f32
            ).astype(bf16)

    early = [k for k in line_a + line_b if k != list(m_copies)[-1]]
    p_first = []
    for turn, k in enumerate([0] + list(m_copies)):
        if turn == n - 1:
            relay_all()
            for k_line in early:
                gradient(k_line, hall.at[k_line - 1])
        spread_all(k).wait_recv()
        part_slots[k] = slots(k)
        d_a, d_b = k // n_b, k % n_b
        for b in range(blocks):
            span = pl.ds(b * block, block)
            value = folded(k, b)
            if k:
                out_a[k, span, :] = value[:, :half_ff].astype(bf16)
                out_b[d_b * n_a + d_a, span, :] = value[:, half_ff:].astype(bf16)
            else:
                own_sum[span, :] = value
        if k == 0:
            gradient(0, hidden_ref)
        if d_a:
            to = back(d_a * n_b)
            p_first.append(send(out_a.at[k], in_a.at[d_a - 1, d_b], first, 0, k, to))
        if d_b:
            source = out_b.at[d_b * n_a + d_a]
            p_first.append(send(source, in_b.at[d_b - 1, d_a], first, 1, k, back(d_b)))

    for k in line_a + line_b:
        if k not in early:
            gradient(k, hall.at[k - 1])
    for k_a in line_a:
        for k_b in line_b:
            for which in range(2):
                d_copies[k_a + k_b, which].wait_recv()
            gradient(k_a + k_b, hall.at[k_a + k_b - 1])

    tile = 64

    def merge(half, level):
        count = half * local * 3
        for i in range(half):
            for e in range(local):

                def body(t, sums, i=i, e=e, half=half):
                    span = pl.ds(pl.multiple_of(t * tile, tile), tile)
                    a = vec[i, e, span, :].astype(f32)
                    b = vec[i + half, e, span, :].astype(f32)
                    return tuple(
                        total + jnp.sum(x.reshape(tile // 8, 8, cols), axis=0)
                        for total, x in zip(sums, (a * b, a * a, b * b))
                    )

                zero = jnp.zeros((8, cols), f32)
                sums = lax.fori_loop(0, ff // tile, body, (zero, zero, zero))
                for m in range(3):
                    narrow = sums[m][:, :128]
                    for c in range(1, cols // 128):
                        narrow = narrow + sums[m][:, c * 128 : (c + 1) * 128]
                    r = (i * local + e) * 3 + m
                    stat[level, pl.ds(r, 1), :] = jnp.sum(narrow, axis=0, keepdims=True)
        copies = []
        for k in range(1, n):
            copy = pltpu.make_async_remote_copy(
                src_ref=stat.at[level],
                dst_ref=stat_in.at[level, k - 1],
                send_sem=s_send.at[level, k - 1],
                recv_sem=s_recv.at[level, k - 1],
                device_id={"dp": near(k)},
                device_id_type=MESH,
            )
            copy.start()
            copies.append(copy)
        for copy in copies:
            copy.wait_recv()
        total = stat[level, :count, :]
        for k in range(1, n):
            total = total + stat_in[level, k - 1, :count, :]
        total = jnp.sum(total, axis=1, keepdims=True)
        for i in range(half):
            for e in range(local):
                r = (i * local + e) * 3
                inner, aa, bb = total[r : r + 1], total[r + 1 : r + 2], total[r + 2 : r + 3]
                coef_a = 1.0 - inner / (2.0 * (aa + epsilon))
                coef_b = 1.0 - inner / (2.0 * (bb + epsilon))

                def mix(t, _, i=i, e=e, half=half, coef_a=coef_a, coef_b=coef_b):
                    span = pl.ds(pl.multiple_of(t * tile, tile), tile)
                    a = vec[i, e, span, :].astype(f32)
                    b = vec[i + half, e, span, :].astype(f32)
                    merged = (coef_a * a + coef_b * b).astype(bf16)
                    if half > 1:
                        vec[i, e, span, :] = merged
                    else:
                        new = w_ref[e, span, :].astype(f32) - learn_rate * merged.astype(f32)
                        nw_ref[e, span, :] = new.astype(bf16)
                    return 0

                lax.fori_loop(0, ff // tile, mix, 0)
        for copy in copies:
            copy.wait_send()

    levels = n.bit_length() - 1
    for level in range(levels - 1):
        merge(n >> level + 1, level)

    for copy in p_first:
        copy.wait_recv()
    p_last = []
    for d in range(1, n_b):
        for b in range(blocks):
            span = pl.ds(b * block, block)
            total = out_a[d, span, :].astype(f32)
            for g in range(n_a - 1):
                total = total + in_a[g, d, span, :].astype(f32)
            next_a[d - 1, span, :] = total.astype(bf16)
        p_last.append(send(next_a.at[d - 1], last_a.at[d - 1], second, 0, d - 1, back(d)))
    for d in range(1, n_a):
        for b in range(blocks):
            span = pl.ds(b * block, block)
            total = out_b[d, span, :].astype(f32)
            for g in range(n_b - 1):
                total = total + in_b[g, d, span, :].astype(f32)
            next_b[d - 1, span, :] = total.astype(bf16)
        p_last.append(send(next_b.at[d - 1], last_b.at[d - 1], second, 1, d - 1, back(d * n_b)))

    merge(1, levels - 1)

    for copy in p_last:
        copy.wait_recv()
    for b in range(blocks):
        span = pl.ds(b * block, block)
        total = own_sum[span, :half_ff]
        for g in range(n_a - 1):
            total = total + in_a[g, 0, span, :].astype(f32)
        for g in range(n_b - 1):
            total = total + last_a[g, span, :].astype(f32)
        gh_ref[span, :half_ff] = total.astype(bf16)
        total = own_sum[span, half_ff:]
        for g in range(n_b - 1):
            total = total + in_b[g, 0, span, :].astype(f32)
        for g in range(n_a - 1):
            total = total + last_b[g, span, :].astype(f32)
        gh_ref[span, half_ff:] = total.astype(bf16)

    for k in range(n):
        spread_all(k).wait_send()
    for group in (m_copies, h_copies, d_copies):
        for copy in group.values():
            copy.wait_send()
    for copy in p_copies:
        copy.wait_send()


def per_device(hidden_rows, grad_send, row_index, block_expert, block_count, down_weight):
    n_e, n = lax.axis_size("expert"), lax.axis_size("dp")
    _, rows, ff = hidden_rows.shape
    width = grad_send.shape[2]
    local, _, cols = down_weight.shape
    cap = rows // n_e
    levels = n.bit_length() - 1
    n_b = 2 ** (n.bit_length() // 2)
    n_a = n // n_b
    stat_rows = -(-(n // 2 * local * 3) // 8) * 8
    vmem = pl.BlockSpec(memory_space=pltpu.VMEM)
    smem = pl.BlockSpec(memory_space=pltpu.SMEM)
    dma = pltpu.SemaphoreType.DMA
    grad_hidden, new_weight = pl.pallas_call(
        functools.partial(kernel, n_e, n),
        out_shape=(
            jax.ShapeDtypeStruct((rows, ff), bf16),
            jax.ShapeDtypeStruct((local, ff, cols), bf16),
        ),
        in_specs=[pl.BlockSpec(memory_space=pl.ANY), vmem, vmem, smem, smem, vmem],
        out_specs=(vmem, vmem),
        scratch_shapes=[
            pltpu.VMEM((n - 1, n_e, cap, cols), bf16),
            pltpu.VMEM((n, n_e, cap, cols), bf16),
            pltpu.VMEM((rows, rows), bf16),
            pltpu.VMEM((n - 1, rows, ff), bf16),
            pltpu.VMEM((n, rows, ff // 2), bf16),
            pltpu.VMEM((n, rows, ff // 2), bf16),
            pltpu.VMEM((n_a - 1, n_b, rows, ff // 2), bf16),
            pltpu.VMEM((n_b - 1, n_a, rows, ff // 2), bf16),
            pltpu.VMEM((n_b - 1, rows, ff // 2), bf16),
            pltpu.VMEM((n_a - 1, rows, ff // 2), bf16),
            pltpu.VMEM((n_b - 1, rows, ff // 2), bf16),
            pltpu.VMEM((n_a - 1, rows, ff // 2), bf16),
            pltpu.VMEM((rows, ff), f32),
            dict(
                slots=pltpu.VMEM((n, rows, cols), bf16),
                vec=pltpu.VMEM((n, local, ff, cols), bf16),
            ),
            pltpu.VMEM((levels, stat_rows, 128), f32),
            pltpu.VMEM((levels, n - 1, stat_rows, 128), f32),
            dma((n,)),
            dma((n,)),
            dma((n - 1,)),
            dma((n - 1,)),
            dma((n - 1,)),
            dma((n - 1,)),
            dma((n - 1, 2)),
            dma((n - 1, 2)),
            dma((2, n)),
            dma((2, n)),
            dma((2, max(n_a, n_b) - 1)),
            dma((2, max(n_a, n_b) - 1)),
            dma((levels, n - 1)),
            dma((levels, n - 1)),
            dma,
        ],
        compiler_params=pltpu.CompilerParams(
            collective_id=0, has_side_effects=True, vmem_limit_bytes=58 * 1024 * 1024
        ),
    )(
        grad_send.reshape(n_e, cap, width),
        hidden_rows[0],
        row_index,
        block_expert[0],
        block_count[0],
        down_weight,
    )
    return grad_hidden[None], new_weight


def solution(mesh):
    in_specs = (
        P("dp", "expert", None),
        P("dp", "expert", None),
        P("expert", None),
        P("expert", None),
        P("expert", None),
        P("expert", None, "dp"),
    )
    out_specs = (P("dp", "expert", None), P("expert", None, "dp"))
    return jax.shard_map(
        per_device, mesh=mesh, in_specs=in_specs, out_specs=out_specs, check_vma=False
    )
```

```python
import functools

import jax
import jax.numpy as jnp
from jax import lax
from jax.experimental import pallas as pl
from jax.experimental.pallas import tpu as pltpu
from jax.sharding import PartitionSpec as P

learn_rate = 0.01
epsilon = 1e-06
MESH = pl.DeviceIdType.MESH
bf16 = jnp.bfloat16
f32 = jnp.float32


def kernel(
    n_e,
    n,
    grad_ref,
    hidden_ref,
    index_ref,
    expert_ref,
    count_ref,
    w_ref,
    gh_ref,
    nw_ref,
    stage,
    part,
    pick,
    hall,
    out_a,
    out_b,
    in_a,
    in_b,
    next_a,
    next_b,
    last_a,
    last_b,
    own_sum,
    v,
    stat,
    stat_in,
    z_send,
    z_recv,
    m_send,
    m_recv,
    h_send,
    h_recv,
    d_send,
    d_recv,
    p_send,
    p_recv,
    q_send,
    q_recv,
    s_send,
    s_recv,
    own_sem,
):
    rows, ff = hidden_ref.shape
    cap = part.shape[2]
    local, _, cols = w_ref.shape
    blocks = expert_ref.shape[0]
    block = rows // blocks
    me_e, me = lax.axis_index("expert"), lax.axis_index("dp")

    def near_e(k):
        return lax.rem(me_e + k + n_e, n_e)

    n_b = 2 ** (n.bit_length() // 2)
    n_a = n // n_b
    me_a, me_b = lax.div(me, n_b), lax.rem(me, n_b)

    def near(k):
        return lax.rem(me_a + k // n_b, n_a) * n_b + lax.rem(me_b + k % n_b, n_b)

    def back(k):
        return lax.rem(me_a + n_a - k // n_b, n_a) * n_b + lax.rem(me_b + n_b - k % n_b, n_b)

    line_a = [d * n_b for d in range(1, n_a)]
    line_b = list(range(1, n_b))

    barrier = pltpu.get_barrier_semaphore()
    for k in range(1, n_e):
        pl.semaphore_signal(barrier, inc=1, device_id={"expert": near_e(k)}, device_id_type=MESH)
    for k in range(1, n):
        pl.semaphore_signal(barrier, inc=1, device_id={"dp": near(k)}, device_id_type=MESH)
    mine = pl.ds(pl.multiple_of(me * cols, cols), cols)
    own = pltpu.make_async_copy(grad_ref.at[me_e, :, mine], part.at[0, me_e], own_sem)
    own.start()
    pl.semaphore_wait(barrier, n_e + n - 2)

    part_e = n_e // 2
    near_base = lax.div(me_e, part_e) * part_e
    bases = (part_e - near_base, near_base)
    place = me_e - near_base
    m_order = line_a + line_b + [a + b for a in line_a for b in line_b]
    m_copies = {}
    for c in range(2):
        for k in m_order:
            to = near(k)
            span = pl.ds(bases[c], part_e)
            m_copies[k, c] = pltpu.make_async_remote_copy(
                src_ref=grad_ref.at[span, :, pl.ds(pl.multiple_of(to * cols, cols), cols)],
                dst_ref=stage.at[k - 1, span],
                send_sem=m_send.at[k - 1, c],
                recv_sem=m_recv.at[k - 1, c],
                device_id={"dp": to},
                device_id_type=MESH,
            )
            m_copies[k, c].start()

    def spread(k, c):
        for j in range(c, part_e):
            to = bases[c] + lax.rem(place + j, part_e)
            pltpu.make_async_remote_copy(
                src_ref=stage.at[k - 1, to] if k else grad_ref.at[to, :, mine],
                dst_ref=part.at[k, me_e],
                send_sem=z_send.at[k],
                recv_sem=z_recv.at[k],
                device_id={"expert": to},
                device_id_type=MESH,
            ).start()

    def spread_all(k):
        others = part.at[k, pl.ds(0, n_e - 1)]
        return pltpu.make_async_remote_copy(
            src_ref=others,
            dst_ref=others,
            send_sem=z_send.at[k],
            recv_sem=z_recv.at[k],
            device_id={"expert": near_e(1)},
            device_id_type=MESH,
        )

    spread(0, 0)
    spread(0, 1)
    h_copies = {}
    for k in line_a + line_b:
        h_copies[k] = pltpu.make_async_remote_copy(
            src_ref=hidden_ref,
            dst_ref=hall.at[k - 1],
            send_sem=h_send.at[k - 1],
            recv_sem=h_recv.at[k - 1],
            device_id={"dp": near(k)},
            device_id_type=MESH,
        )
    d_copies = {}

    def relay(k, source, to, which):
        span = pl.ds(which * (rows // 2), rows // 2)
        copy = pltpu.make_async_remote_copy(
            src_ref=hall.at[source - 1, span],
            dst_ref=hall.at[k - 1, span],
            send_sem=d_send.at[k - 1, which],
            recv_sem=d_recv.at[k - 1, which],
            device_id={"dp": near(to)},
            device_id_type=MESH,
        )
        copy.start()
        d_copies[k, which] = copy

    received = lax.broadcasted_iota(jnp.int32, (rows, rows), 0)
    hits = jnp.where(index_ref[...] == received, 1.0, 0.0).astype(f32).T
    for b in range(blocks):
        slot = lax.broadcasted_iota(jnp.int32, (block, rows), 0)
        live = jnp.where(slot < count_ref[b], hits[b * block : (b + 1) * block], 0.0)
        pick[pl.ds(b * block, block), :] = live.astype(bf16)

    for c in range(2):
        for k in m_order:
            m_copies[k, c].wait_recv()
            spread(k, c)
            if c:
                part[k, me_e] = stage[k - 1, me_e]
    for k in h_copies:
        h_copies[k].start()
    own.wait()

    def relay_all():
        for k_a in line_a:
            h_copies[k_a].wait_recv()
            for k_b in line_b:
                relay(k_a + k_b, k_a, k_b, 0)
        for k_b in line_b:
            h_copies[k_b].wait_recv()
            for k_a in line_a:
                relay(k_a + k_b, k_b, k_a, 1)

    def slots(k):
        flat = part[k].reshape(rows, cols)
        return jnp.dot(pick[...], flat, preferred_element_type=f32).astype(bf16)

    def folded(k, b):
        return lax.dot_general(
            part_slots[k, pl.ds(b * block, block), :],
            w_ref[expert_ref[b]],
            (((1,), (1,)), ((), ())),
            preferred_element_type=f32,
        )

    part_slots = v["slots"]
    vec = v["vec"]

    p_copies = []
    half_ff = ff // 2

    def send(src, dst, sems, side, d, to):
        copy = pltpu.make_async_remote_copy(
            src_ref=src,
            dst_ref=dst,
            send_sem=sems[0].at[side, d],
            recv_sem=sems[1].at[side, d],
            device_id={"dp": to},
            device_id_type=MESH,
        )
        copy.start()
        p_copies.append(copy)
        return copy

    first, second = (p_send, p_recv), (q_send, q_recv)
    def gradient(k, hidden):
        for e in range(local):
            pieces = [
                jnp.where(expert_ref[b] == e, hidden[pl.ds(b * block, block), :], jnp.zeros((), bf16))
                for b in range(blocks)
            ]
            chosen = jnp.concatenate(pieces, axis=0)
            vec[back(k), e] = lax.dot_general(
                chosen, part_slots[k], (((0,), (0,)), ((), ())), preferred_element_type=f32
            ).astype(bf16)

    early = [k for k in line_a + line_b if k != m_order[-1]]
    p_first = []
    for turn, k in enumerate([0] + m_order):
        if turn == n - 1:
            relay_all()
            for k_line in early:
                gradient(k_line, hall.at[k_line - 1])
        spread_all(k).wait_recv()
        part_slots[k] = slots(k)
        d_a, d_b = k // n_b, k % n_b
        for b in range(blocks):
            span = pl.ds(b * block, block)
            value = folded(k, b)
            if k:
                out_a[k, span, :] = value[:, :half_ff].astype(bf16)
                out_b[d_b * n_a + d_a, span, :] = value[:, half_ff:].astype(bf16)
            else:
                own_sum[span, :] = value
        if k == 0:
            gradient(0, hidden_ref)
        if d_a:
            to = back(d_a * n_b)
            p_first.append(send(out_a.at[k], in_a.at[d_a - 1, d_b], first, 0, k, to))
        if d_b:
            source = out_b.at[d_b * n_a + d_a]
            p_first.append(send(source, in_b.at[d_b - 1, d_a], first, 1, k, back(d_b)))

    for k in line_a + line_b:
        if k not in early:
            gradient(k, hall.at[k - 1])
    for k_a in line_a:
        for k_b in line_b:
            for which in range(2):
                d_copies[k_a + k_b, which].wait_recv()
            gradient(k_a + k_b, hall.at[k_a + k_b - 1])

    tile = 64

    def merge(half, level):
        count = half * local * 3
        for i in range(half):
            for e in range(local):

                def body(t, sums, i=i, e=e, half=half):
                    span = pl.ds(pl.multiple_of(t * tile, tile), tile)
                    a = vec[i, e, span, :].astype(f32)
                    b = vec[i + half, e, span, :].astype(f32)
                    return tuple(
                        total + jnp.sum(x.reshape(tile // 8, 8, cols), axis=0)
                        for total, x in zip(sums, (a * b, a * a, b * b))
                    )

                zero = jnp.zeros((8, cols), f32)
                sums = lax.fori_loop(0, ff // tile, body, (zero, zero, zero))
                for m in range(3):
                    narrow = sums[m][:, :128]
                    for c in range(1, cols // 128):
                        narrow = narrow + sums[m][:, c * 128 : (c + 1) * 128]
                    r = (i * local + e) * 3 + m
                    stat[level, pl.ds(r, 1), :] = jnp.sum(narrow, axis=0, keepdims=True)
        copies = []
        for k in range(1, n):
            copy = pltpu.make_async_remote_copy(
                src_ref=stat.at[level],
                dst_ref=stat_in.at[level, k - 1],
                send_sem=s_send.at[level, k - 1],
                recv_sem=s_recv.at[level, k - 1],
                device_id={"dp": near(k)},
                device_id_type=MESH,
            )
            copy.start()
            copies.append(copy)
        for copy in copies:
            copy.wait_recv()
        total = stat[level, :count, :]
        for k in range(1, n):
            total = total + stat_in[level, k - 1, :count, :]
        total = jnp.sum(total, axis=1, keepdims=True)
        for i in range(half):
            for e in range(local):
                r = (i * local + e) * 3
                inner, aa, bb = total[r : r + 1], total[r + 1 : r + 2], total[r + 2 : r + 3]
                coef_a = 1.0 - inner / (2.0 * (aa + epsilon))
                coef_b = 1.0 - inner / (2.0 * (bb + epsilon))

                def mix(t, _, i=i, e=e, half=half, coef_a=coef_a, coef_b=coef_b):
                    span = pl.ds(pl.multiple_of(t * tile, tile), tile)
                    a = vec[i, e, span, :].astype(f32)
                    b = vec[i + half, e, span, :].astype(f32)
                    merged = (coef_a * a + coef_b * b).astype(bf16)
                    if half > 1:
                        vec[i, e, span, :] = merged
                    else:
                        new = w_ref[e, span, :].astype(f32) - learn_rate * merged.astype(f32)
                        nw_ref[e, span, :] = new.astype(bf16)
                    return 0

                lax.fori_loop(0, ff // tile, mix, 0)
        for copy in copies:
            copy.wait_send()

    levels = n.bit_length() - 1
    for level in range(levels - 1):
        merge(n >> level + 1, level)

    for copy in p_first:
        copy.wait_recv()
    p_last = []
    for d in range(1, n_b):
        for b in range(blocks):
            span = pl.ds(b * block, block)
            total = out_a[d, span, :].astype(f32)
            for g in range(n_a - 1):
                total = total + in_a[g, d, span, :].astype(f32)
            next_a[d - 1, span, :] = total.astype(bf16)
        p_last.append(send(next_a.at[d - 1], last_a.at[d - 1], second, 0, d - 1, back(d)))
    for d in range(1, n_a):
        for b in range(blocks):
            span = pl.ds(b * block, block)
            total = out_b[d, span, :].astype(f32)
            for g in range(n_b - 1):
                total = total + in_b[g, d, span, :].astype(f32)
            next_b[d - 1, span, :] = total.astype(bf16)
        p_last.append(send(next_b.at[d - 1], last_b.at[d - 1], second, 1, d - 1, back(d * n_b)))

    merge(1, levels - 1)

    for copy in p_last:
        copy.wait_recv()
    for b in range(blocks):
        span = pl.ds(b * block, block)
        total = own_sum[span, :half_ff]
        for g in range(n_a - 1):
            total = total + in_a[g, 0, span, :].astype(f32)
        for g in range(n_b - 1):
            total = total + last_a[g, span, :].astype(f32)
        gh_ref[span, :half_ff] = total.astype(bf16)
        total = own_sum[span, half_ff:]
        for g in range(n_b - 1):
            total = total + in_b[g, 0, span, :].astype(f32)
        for g in range(n_a - 1):
            total = total + last_b[g, span, :].astype(f32)
        gh_ref[span, half_ff:] = total.astype(bf16)

    for k in range(n):
        spread_all(k).wait_send()
    for group in (m_copies, h_copies, d_copies):
        for copy in group.values():
            copy.wait_send()
    for copy in p_copies:
        copy.wait_send()


def per_device(hidden_rows, grad_send, row_index, block_expert, block_count, down_weight):
    n_e, n = lax.axis_size("expert"), lax.axis_size("dp")
    _, rows, ff = hidden_rows.shape
    width = grad_send.shape[2]
    local, _, cols = down_weight.shape
    cap = rows // n_e
    levels = n.bit_length() - 1
    n_b = 2 ** (n.bit_length() // 2)
    n_a = n // n_b
    stat_rows = -(-(n // 2 * local * 3) // 8) * 8
    vmem = pl.BlockSpec(memory_space=pltpu.VMEM)
    smem = pl.BlockSpec(memory_space=pltpu.SMEM)
    dma = pltpu.SemaphoreType.DMA
    grad_hidden, new_weight = pl.pallas_call(
        functools.partial(kernel, n_e, n),
        out_shape=(
            jax.ShapeDtypeStruct((rows, ff), bf16),
            jax.ShapeDtypeStruct((local, ff, cols), bf16),
        ),
        in_specs=[pl.BlockSpec(memory_space=pl.ANY), vmem, vmem, smem, smem, vmem],
        out_specs=(vmem, vmem),
        scratch_shapes=[
            pltpu.VMEM((n - 1, n_e, cap, cols), bf16),
            pltpu.VMEM((n, n_e, cap, cols), bf16),
            pltpu.VMEM((rows, rows), bf16),
            pltpu.VMEM((n - 1, rows, ff), bf16),
            pltpu.VMEM((n, rows, ff // 2), bf16),
            pltpu.VMEM((n, rows, ff // 2), bf16),
            pltpu.VMEM((n_a - 1, n_b, rows, ff // 2), bf16),
            pltpu.VMEM((n_b - 1, n_a, rows, ff // 2), bf16),
            pltpu.VMEM((n_b - 1, rows, ff // 2), bf16),
            pltpu.VMEM((n_a - 1, rows, ff // 2), bf16),
            pltpu.VMEM((n_b - 1, rows, ff // 2), bf16),
            pltpu.VMEM((n_a - 1, rows, ff // 2), bf16),
            pltpu.VMEM((rows, ff), f32),
            dict(
                slots=pltpu.VMEM((n, rows, cols), bf16),
                vec=pltpu.VMEM((n, local, ff, cols), bf16),
            ),
            pltpu.VMEM((levels, stat_rows, 128), f32),
            pltpu.VMEM((levels, n - 1, stat_rows, 128), f32),
            dma((n,)),
            dma((n,)),
            dma((n - 1, 2)),
            dma((n - 1, 2)),
            dma((n - 1,)),
            dma((n - 1,)),
            dma((n - 1, 2)),
            dma((n - 1, 2)),
            dma((2, n)),
            dma((2, n)),
            dma((2, max(n_a, n_b) - 1)),
            dma((2, max(n_a, n_b) - 1)),
            dma((levels, n - 1)),
            dma((levels, n - 1)),
            dma,
        ],
        compiler_params=pltpu.CompilerParams(
            collective_id=0, has_side_effects=True, vmem_limit_bytes=58 * 1024 * 1024
        ),
    )(
        grad_send.reshape(n_e, cap, width),
        hidden_rows[0],
        row_index,
        block_expert[0],
        block_count[0],
        down_weight,
    )
    return grad_hidden[None], new_weight


def solution(mesh):
    in_specs = (
        P("dp", "expert", None),
        P("dp", "expert", None),
        P("expert", None),
        P("expert", None),
        P("expert", None),
        P("expert", None, "dp"),
    )
    out_specs = (P("dp", "expert", None), P("expert", None, "dp"))
    return jax.shard_map(
        per_device, mesh=mesh, in_specs=in_specs, out_specs=out_specs, check_vma=False
    )
```

```python
import functools

import jax
import jax.numpy as jnp
from jax import lax
from jax.experimental import pallas as pl
from jax.experimental.pallas import tpu as pltpu
from jax.sharding import PartitionSpec as P

learn_rate = 0.01
epsilon = 1e-06
MESH = pl.DeviceIdType.MESH
bf16 = jnp.bfloat16
f32 = jnp.float32


def kernel(
    n_e,
    n,
    grad_ref,
    hidden_ref,
    index_ref,
    expert_ref,
    count_ref,
    w_ref,
    gh_ref,
    nw_ref,
    stage,
    part,
    pick,
    hall,
    out_a,
    out_b,
    in_a,
    in_b,
    next_a,
    next_b,
    last_a,
    last_b,
    own_sum,
    v,
    stat,
    stat_in,
    z_send,
    z_recv,
    m_send,
    m_recv,
    h_send,
    h_recv,
    d_send,
    d_recv,
    p_send,
    p_recv,
    q_send,
    q_recv,
    s_send,
    s_recv,
    own_sem,
):
    rows, ff = hidden_ref.shape
    cap = part.shape[2]
    local, _, cols = w_ref.shape
    blocks = expert_ref.shape[0]
    block = rows // blocks
    me_e, me = lax.axis_index("expert"), lax.axis_index("dp")

    def near_e(k):
        return lax.rem(me_e + k + n_e, n_e)

    n_b = 2 ** (n.bit_length() // 2)
    n_a = n // n_b
    me_a, me_b = lax.div(me, n_b), lax.rem(me, n_b)

    def near(k):
        return lax.rem(me_a + k // n_b, n_a) * n_b + lax.rem(me_b + k % n_b, n_b)

    def back(k):
        return lax.rem(me_a + n_a - k // n_b, n_a) * n_b + lax.rem(me_b + n_b - k % n_b, n_b)

    line_a = [d * n_b for d in range(1, n_a)]
    line_b = list(range(1, n_b))

    barrier = pltpu.get_barrier_semaphore()
    for k in range(1, n_e):
        pl.semaphore_signal(barrier, inc=1, device_id={"expert": near_e(k)}, device_id_type=MESH)
    for k in range(1, n):
        pl.semaphore_signal(barrier, inc=1, device_id={"dp": near(k)}, device_id_type=MESH)
    mine = pl.ds(pl.multiple_of(me * cols, cols), cols)
    own = pltpu.make_async_copy(grad_ref.at[me_e, :, mine], part.at[0, me_e], own_sem)
    own.start()
    pl.semaphore_wait(barrier, n_e + n - 2)

    part_e = n_e // 2
    near_base = lax.div(me_e, part_e) * part_e
    bases = (part_e - near_base, near_base)
    place = me_e - near_base
    m_order = line_a + line_b + [a + b for a in line_a for b in line_b]
    m_copies = {}
    for c in range(2):
        for k in m_order:
            to = near(k)
            span = pl.ds(bases[c], part_e)
            m_copies[k, c] = pltpu.make_async_remote_copy(
                src_ref=grad_ref.at[span, :, pl.ds(pl.multiple_of(to * cols, cols), cols)],
                dst_ref=stage.at[k - 1, span],
                send_sem=m_send.at[k - 1, c],
                recv_sem=m_recv.at[k - 1, c],
                device_id={"dp": to},
                device_id_type=MESH,
            )
            m_copies[k, c].start()

    def spread(k, c):
        for j in range(c, part_e):
            to = bases[c] + lax.rem(place + j, part_e)
            pltpu.make_async_remote_copy(
                src_ref=stage.at[k - 1, to] if k else grad_ref.at[to, :, mine],
                dst_ref=part.at[k, me_e],
                send_sem=z_send.at[k],
                recv_sem=z_recv.at[k],
                device_id={"expert": to},
                device_id_type=MESH,
            ).start()

    def spread_all(k):
        others = part.at[k, pl.ds(0, n_e - 1)]
        return pltpu.make_async_remote_copy(
            src_ref=others,
            dst_ref=others,
            send_sem=z_send.at[k],
            recv_sem=z_recv.at[k],
            device_id={"expert": near_e(1)},
            device_id_type=MESH,
        )

    spread(0, 0)
    spread(0, 1)
    h_copies = {}
    for k in line_a + line_b:
        h_copies[k] = pltpu.make_async_remote_copy(
            src_ref=hidden_ref,
            dst_ref=hall.at[k - 1],
            send_sem=h_send.at[k - 1],
            recv_sem=h_recv.at[k - 1],
            device_id={"dp": near(k)},
            device_id_type=MESH,
        )
    d_copies = {}

    def relay(k, source, to, which):
        span = pl.ds(which * (rows // 2), rows // 2)
        copy = pltpu.make_async_remote_copy(
            src_ref=hall.at[source - 1, span],
            dst_ref=hall.at[k - 1, span],
            send_sem=d_send.at[k - 1, which],
            recv_sem=d_recv.at[k - 1, which],
            device_id={"dp": near(to)},
            device_id_type=MESH,
        )
        copy.start()
        d_copies[k, which] = copy

    received = lax.broadcasted_iota(jnp.int32, (rows, rows), 0)
    hits = jnp.where(index_ref[...] == received, 1.0, 0.0).astype(f32).T
    for b in range(blocks):
        slot = lax.broadcasted_iota(jnp.int32, (block, rows), 0)
        live = jnp.where(slot < count_ref[b], hits[b * block : (b + 1) * block], 0.0)
        pick[pl.ds(b * block, block), :] = live.astype(bf16)

    for c in range(2):
        for k in m_order:
            m_copies[k, c].wait_recv()
            spread(k, c)
            if c:
                part[k, me_e] = stage[k - 1, me_e]
    for k in h_copies:
        h_copies[k].start()
    own.wait()

    def relay_all():
        for k_a in line_a:
            h_copies[k_a].wait_recv()
            for k_b in line_b:
                relay(k_a + k_b, k_a, k_b, 0)
        for k_b in line_b:
            h_copies[k_b].wait_recv()
            for k_a in line_a:
                relay(k_a + k_b, k_b, k_a, 1)

    def slots(k):
        flat = part[k].reshape(rows, cols)
        return jnp.dot(pick[...], flat, preferred_element_type=f32).astype(bf16)

    def folded(k, b):
        return lax.dot_general(
            part_slots[k, pl.ds(b * block, block), :],
            w_ref[expert_ref[b]],
            (((1,), (1,)), ((), ())),
            preferred_element_type=f32,
        )

    part_slots = v["slots"]
    vec = v["vec"]

    p_copies = []
    half_ff = ff // 2

    def send(src, dst, sems, side, d, to):
        copy = pltpu.make_async_remote_copy(
            src_ref=src,
            dst_ref=dst,
            send_sem=sems[0].at[side, d],
            recv_sem=sems[1].at[side, d],
            device_id={"dp": to},
            device_id_type=MESH,
        )
        copy.start()
        p_copies.append(copy)
        return copy

    first, second = (p_send, p_recv), (q_send, q_recv)
    def gradient(k, hidden):
        for e in range(local):
            pieces = [
                jnp.where(expert_ref[b] == e, hidden[pl.ds(b * block, block), :], jnp.zeros((), bf16))
                for b in range(blocks)
            ]
            chosen = jnp.concatenate(pieces, axis=0)
            vec[back(k), e] = lax.dot_general(
                chosen, part_slots[k], (((0,), (0,)), ((), ())), preferred_element_type=f32
            ).astype(bf16)

    p_first = []
    for turn, k in enumerate([0] + m_order):
        if turn == n - 1:
            relay_all()
        spread_all(k).wait_recv()
        part_slots[k] = slots(k)
        d_a, d_b = k // n_b, k % n_b
        for b in range(blocks):
            span = pl.ds(b * block, block)
            value = folded(k, b)
            if k:
                out_a[k, span, :] = value[:, :half_ff].astype(bf16)
                out_b[d_b * n_a + d_a, span, :] = value[:, half_ff:].astype(bf16)
            else:
                own_sum[span, :] = value
        if k == 0:
            gradient(0, hidden_ref)
        if d_a:
            to = back(d_a * n_b)
            p_first.append(send(out_a.at[k], in_a.at[d_a - 1, d_b], first, 0, k, to))
        if d_b:
            source = out_b.at[d_b * n_a + d_a]
            p_first.append(send(source, in_b.at[d_b - 1, d_a], first, 1, k, back(d_b)))

    for k in line_a + line_b:
        gradient(k, hall.at[k - 1])
    for k_a in line_a:
        for k_b in line_b:
            for which in range(2):
                d_copies[k_a + k_b, which].wait_recv()
            gradient(k_a + k_b, hall.at[k_a + k_b - 1])

    tile = 64

    def merge(half, level):
        count = half * local * 3
        for i in range(half):
            for e in range(local):

                def body(t, sums, i=i, e=e, half=half):
                    span = pl.ds(pl.multiple_of(t * tile, tile), tile)
                    a = vec[i, e, span, :].astype(f32)
                    b = vec[i + half, e, span, :].astype(f32)
                    return tuple(
                        total + jnp.sum(x.reshape(tile // 8, 8, cols), axis=0)
                        for total, x in zip(sums, (a * b, a * a, b * b))
                    )

                zero = jnp.zeros((8, cols), f32)
                sums = lax.fori_loop(0, ff // tile, body, (zero, zero, zero))
                for m in range(3):
                    narrow = sums[m][:, :128]
                    for c in range(1, cols // 128):
                        narrow = narrow + sums[m][:, c * 128 : (c + 1) * 128]
                    r = (i * local + e) * 3 + m
                    stat[level, pl.ds(r, 1), :] = jnp.sum(narrow, axis=0, keepdims=True)
        copies = []
        for k in range(1, n):
            copy = pltpu.make_async_remote_copy(
                src_ref=stat.at[level],
                dst_ref=stat_in.at[level, k - 1],
                send_sem=s_send.at[level, k - 1],
                recv_sem=s_recv.at[level, k - 1],
                device_id={"dp": near(k)},
                device_id_type=MESH,
            )
            copy.start()
            copies.append(copy)
        for copy in copies:
            copy.wait_recv()
        total = stat[level, :count, :]
        for k in range(1, n):
            total = total + stat_in[level, k - 1, :count, :]
        total = jnp.sum(total, axis=1, keepdims=True)
        for i in range(half):
            for e in range(local):
                r = (i * local + e) * 3
                inner, aa, bb = total[r : r + 1], total[r + 1 : r + 2], total[r + 2 : r + 3]
                coef_a = 1.0 - inner / (2.0 * (aa + epsilon))
                coef_b = 1.0 - inner / (2.0 * (bb + epsilon))

                def mix(t, _, i=i, e=e, half=half, coef_a=coef_a, coef_b=coef_b):
                    span = pl.ds(pl.multiple_of(t * tile, tile), tile)
                    a = vec[i, e, span, :].astype(f32)
                    b = vec[i + half, e, span, :].astype(f32)
                    merged = (coef_a * a + coef_b * b).astype(bf16)
                    if half > 1:
                        vec[i, e, span, :] = merged
                    else:
                        new = w_ref[e, span, :].astype(f32) - learn_rate * merged.astype(f32)
                        nw_ref[e, span, :] = new.astype(bf16)
                    return 0

                lax.fori_loop(0, ff // tile, mix, 0)
        for copy in copies:
            copy.wait_send()

    levels = n.bit_length() - 1
    for level in range(levels - 1):
        merge(n >> level + 1, level)

    for copy in p_first:
        copy.wait_recv()
    p_last = []
    for d in range(1, n_b):
        for b in range(blocks):
            span = pl.ds(b * block, block)
            total = out_a[d, span, :].astype(f32)
            for g in range(n_a - 1):
                total = total + in_a[g, d, span, :].astype(f32)
            next_a[d - 1, span, :] = total.astype(bf16)
        p_last.append(send(next_a.at[d - 1], last_a.at[d - 1], second, 0, d - 1, back(d)))
    for d in range(1, n_a):
        for b in range(blocks):
            span = pl.ds(b * block, block)
            total = out_b[d, span, :].astype(f32)
            for g in range(n_b - 1):
                total = total + in_b[g, d, span, :].astype(f32)
            next_b[d - 1, span, :] = total.astype(bf16)
        p_last.append(send(next_b.at[d - 1], last_b.at[d - 1], second, 1, d - 1, back(d * n_b)))

    merge(1, levels - 1)

    for copy in p_last:
        copy.wait_recv()
    for b in range(blocks):
        span = pl.ds(b * block, block)
        total = own_sum[span, :half_ff]
        for g in range(n_a - 1):
            total = total + in_a[g, 0, span, :].astype(f32)
        for g in range(n_b - 1):
            total = total + last_a[g, span, :].astype(f32)
        gh_ref[span, :half_ff] = total.astype(bf16)
        total = own_sum[span, half_ff:]
        for g in range(n_b - 1):
            total = total + in_b[g, 0, span, :].astype(f32)
        for g in range(n_a - 1):
            total = total + last_b[g, span, :].astype(f32)
        gh_ref[span, half_ff:] = total.astype(bf16)

    for k in range(n):
        spread_all(k).wait_send()
    for group in (m_copies, h_copies, d_copies):
        for copy in group.values():
            copy.wait_send()
    for copy in p_copies:
        copy.wait_send()


def per_device(hidden_rows, grad_send, row_index, block_expert, block_count, down_weight):
    n_e, n = lax.axis_size("expert"), lax.axis_size("dp")
    _, rows, ff = hidden_rows.shape
    width = grad_send.shape[2]
    local, _, cols = down_weight.shape
    cap = rows // n_e
    levels = n.bit_length() - 1
    n_b = 2 ** (n.bit_length() // 2)
    n_a = n // n_b
    stat_rows = -(-(n // 2 * local * 3) // 8) * 8
    vmem = pl.BlockSpec(memory_space=pltpu.VMEM)
    smem = pl.BlockSpec(memory_space=pltpu.SMEM)
    dma = pltpu.SemaphoreType.DMA
    grad_hidden, new_weight = pl.pallas_call(
        functools.partial(kernel, n_e, n),
        out_shape=(
            jax.ShapeDtypeStruct((rows, ff), bf16),
            jax.ShapeDtypeStruct((local, ff, cols), bf16),
        ),
        in_specs=[pl.BlockSpec(memory_space=pl.ANY), vmem, vmem, smem, smem, vmem],
        out_specs=(vmem, vmem),
        scratch_shapes=[
            pltpu.VMEM((n - 1, n_e, cap, cols), bf16),
            pltpu.VMEM((n, n_e, cap, cols), bf16),
            pltpu.VMEM((rows, rows), bf16),
            pltpu.VMEM((n - 1, rows, ff), bf16),
            pltpu.VMEM((n, rows, ff // 2), bf16),
            pltpu.VMEM((n, rows, ff // 2), bf16),
            pltpu.VMEM((n_a - 1, n_b, rows, ff // 2), bf16),
            pltpu.VMEM((n_b - 1, n_a, rows, ff // 2), bf16),
            pltpu.VMEM((n_b - 1, rows, ff // 2), bf16),
            pltpu.VMEM((n_a - 1, rows, ff // 2), bf16),
            pltpu.VMEM((n_b - 1, rows, ff // 2), bf16),
            pltpu.VMEM((n_a - 1, rows, ff // 2), bf16),
            pltpu.VMEM((rows, ff), f32),
            dict(
                slots=pltpu.VMEM((n, rows, cols), bf16),
                vec=pltpu.VMEM((n, local, ff, cols), bf16),
            ),
            pltpu.VMEM((levels, stat_rows, 128), f32),
            pltpu.VMEM((levels, n - 1, stat_rows, 128), f32),
            dma((n,)),
            dma((n,)),
            dma((n - 1, 2)),
            dma((n - 1, 2)),
            dma((n - 1,)),
            dma((n - 1,)),
            dma((n - 1, 2)),
            dma((n - 1, 2)),
            dma((2, n)),
            dma((2, n)),
            dma((2, max(n_a, n_b) - 1)),
            dma((2, max(n_a, n_b) - 1)),
            dma((levels, n - 1)),
            dma((levels, n - 1)),
            dma,
        ],
        compiler_params=pltpu.CompilerParams(
            collective_id=0, has_side_effects=True, vmem_limit_bytes=58 * 1024 * 1024
        ),
    )(
        grad_send.reshape(n_e, cap, width),
        hidden_rows[0],
        row_index,
        block_expert[0],
        block_count[0],
        down_weight,
    )
    return grad_hidden[None], new_weight


def solution(mesh):
    in_specs = (
        P("dp", "expert", None),
        P("dp", "expert", None),
        P("expert", None),
        P("expert", None),
        P("expert", None),
        P("expert", None, "dp"),
    )
    out_specs = (P("dp", "expert", None), P("expert", None, "dp"))
    return jax.shard_map(
        per_device, mesh=mesh, in_specs=in_specs, out_specs=out_specs, check_vma=False
    )
```
